32 devices in a mesh: adv: 2 (over y), imp: 16 (over z, x, core).
Axes of the slice: x: 2, y: 2, z: 4, core: 2. Of those that a mesh axis runs over, the one named last changes fastest.
Arguments:
- adv_embed: float32 [4096, 64], P(('adv', 'imp')), may hold values from -5 to 5
- imp_embed: float32 [8192, 64], P(('imp', 'adv')), may hold values from -5 to 5
- value_scale: float32 [4096], P('adv'), may hold values from 0.3 to 3
- spend_class: int32 [4096], P('adv'), may hold values from 0 to 7
- eligible: int32 [32, 64], P('adv', 'imp'), may hold values from 0 to 1, as said below
Outputs:
- bid_density: float32 [4096, 8192], P('adv', 'imp')
- prices: float32 [8192], P('imp')
- pacing: float32 [4096], P('adv')
The draws below stay inside these ranges and needn't reach their ends.
Inputs may be any that keep to these rules, and one draw needn't show every extreme that they name: Every impression block is eligible for at least one advertiser block.
All inputs are finite; a program needn't handle non-finite values.
Results may differ from the reference program's by a relative error of at most 0.0002.
Values sent between devices are 32-bit elements; how exact they have to be, the bound alone decides.
No kernel may reach another device: no remote copies, remote signals or barrier semaphores. Data moves between devices by JAX's collectives and lax.ppermute only.
A program may use at most 64 MiB of HBM per device.

```python
import math
import jax
import jax.numpy as jnp
from jax import lax

EMB = 64
BLOCK = 128
ITERS = 2
ADV_DEV = 2048
ADVS = 4096
IMPS = 8192
N_ADV = 2


def draw_eligible(key, part):
    block_rows = ADVS // BLOCK
    block_cols = IMPS // BLOCK
    random_bits = jax.random.randint(key, (block_rows, block_cols), 0, 2, dtype=jnp.int32)
    row_index = jnp.arange(block_rows, dtype=jnp.int32)[:, None]
    col_index = jnp.arange(block_cols, dtype=jnp.int32)[None, :]
    forced = (row_index == col_index % block_rows).astype(jnp.int32)
    return jnp.maximum(random_bits, forced).astype(jnp.int32)


def with_ends(drawn, own_key, least, top_value):
    longest = drawn.shape.index(max(drawn.shape))
    spots = []
    for shift in (0, 1):
        where = [jax.random.randint(jax.random.fold_in(own_key, axis), (), 0, length) for axis, length in enumerate(drawn.shape)]
        where[longest] = (where[longest] + shift) % drawn.shape[longest]
        spots.append(tuple(where))
    return drawn.at[spots[0]].set(least).at[spots[1]].set(top_value)


def block_levels(key, shape, shards, low, high):
    def one(dim, blocks):
        steps = jax.random.uniform(jax.random.fold_in(jax.random.fold_in(key, 6), dim), (blocks,), jnp.float32, low / len(shards), high / len(shards))
        return jnp.repeat(jnp.exp(steps), shape[dim] // blocks).reshape((-1,) + (1,) * (len(shape) - dim - 1))

    level = one(*shards[0])
    for cut in shards[1:]:
        level = level * one(*cut)
    return level


def gaussian(key, extent, deviation, reach, split=(), held_as=jnp.bfloat16):
    entries = deviation * jax.random.normal(key, extent, jnp.float32)
    if split:
        entries = entries * block_levels(key, extent, split, -0.22, 0.18)
    return jnp.clip(entries, -reach, reach).astype(held_as)


def setup_inputs(seed: int = 0) -> dict:
    arg_keys = jax.random.split(jax.random.key(seed), 6)
    adv_embed = gaussian(arg_keys[0], (ADVS, EMB), 1.0, 5.0, ((0, 32),), jnp.float32)
    imp_embed = gaussian(arg_keys[1], (IMPS, EMB), 1.0, 5.0, ((0, 32),), jnp.float32)
    value_scale = jnp.clip(jnp.exp(math.log(3.0) - 2.3025851 * jax.random.uniform(arg_keys[2], (ADVS,), jnp.float32) ** block_levels(arg_keys[2], (ADVS,), ((0, 2),), -0.2, 0.2)), 0.3, 3.0)
    spend_class = with_ends(jax.random.randint(arg_keys[3], (ADVS,), 0, 8), jax.random.fold_in(arg_keys[3], 1), 0, 7).astype(jnp.int32)
    eligible = draw_eligible(jax.random.fold_in(arg_keys[5], 71), 0)
    return {"adv_embed": adv_embed, "imp_embed": imp_embed, "value_scale": value_scale, "spend_class": spend_class, "eligible": eligible}


score_gain = 0.0875


def block_values(embed_rows, scale_rows, mask_rows, imp_embed):
    scores = jnp.einsum("ae,ie->ai", embed_rows, imp_embed, precision=lax.Precision.HIGHEST, preferred_element_type=jnp.float32) * score_gain
    count_rows = mask_rows.shape[0]
    count_cols = mask_rows.shape[1]
    expanded = jnp.broadcast_to(mask_rows.astype(jnp.float32)[:, None, :, None], (count_rows, BLOCK, count_cols, BLOCK))
    blocks_mask = expanded.reshape(count_rows * BLOCK, count_cols * BLOCK)
    values = scale_rows[:, None] * jnp.exp(scores) * blocks_mask
    return values, blocks_mask


def block_bids(embed_rows, scale_rows, mask_rows, limit_rows, adv_factor, imp_factor, power, imp_embed):
    values, blocks_mask = block_values(embed_rows, scale_rows, mask_rows, imp_embed)
    bid_tile = blocks_mask * limit_rows[:, None] / IMPS
    for step in range(power):
        bid_tile = bid_tile * values
    bid_tile = bid_tile * adv_factor[:, None] / imp_factor[None, :]
    return values, bid_tile


def reference(adv_embed, imp_embed, value_scale, spend_class, eligible):
    allowance = (IMPS / ADVS) * jnp.exp(0.3 * spend_class.astype(jnp.float32) - 1.2)
    embed_groups = adv_embed.reshape(N_ADV, ADV_DEV, EMB)
    scale_groups = value_scale.reshape(N_ADV, ADV_DEV)
    limit_groups = allowance.reshape(N_ADV, ADV_DEV)
    mask_groups = eligible.reshape(N_ADV, ADV_DEV // BLOCK, IMPS // BLOCK)
    adv_factor = jnp.ones((N_ADV, ADV_DEV), jnp.float32)
    imp_factor = jnp.ones((IMPS,), jnp.float32)
    prices = jnp.ones((IMPS,), jnp.float32)
    pacing_groups = jnp.ones((N_ADV, ADV_DEV), jnp.float32)
    for power in range(ITERS):
        def column_sums(packed, power=power, imp_factor=imp_factor):
            values, bid_tile = block_bids(packed[0], packed[1], packed[2], packed[3], packed[4], imp_factor, power, imp_embed)
            return jnp.sum(bid_tile, axis=0)

        prices = jnp.sum(lax.map(column_sums, (embed_groups, scale_groups, mask_groups, limit_groups, adv_factor)), axis=0)

        def row_sums(packed, power=power, imp_factor=imp_factor, prices=prices):
            values, bid_tile = block_bids(packed[0], packed[1], packed[2], packed[3], packed[4], imp_factor, power, imp_embed)
            gain = values * bid_tile / prices[None, :]
            return jnp.sum(gain, axis=1)

        spending = lax.map(row_sums, (embed_groups, scale_groups, mask_groups, limit_groups, adv_factor))
        pacing_groups = limit_groups / jnp.maximum(spending, limit_groups)
        adv_factor = adv_factor * pacing_groups
        imp_factor = imp_factor * prices

    def final_bids(packed):
        values, bid_tile = block_bids(packed[0], packed[1], packed[2], packed[3], packed[4], imp_factor, ITERS, imp_embed)
        return bid_tile * ADVS

    density = lax.map(final_bids, (embed_groups, scale_groups, mask_groups, limit_groups, adv_factor))
    return density.reshape(ADVS, IMPS), prices, pacing_groups.reshape(ADVS)
```

```python
import math

import jax
import jax.numpy as jnp
from jax import lax
from jax.experimental import pallas as pl
from jax.experimental.pallas import tpu as pltpu
from jax.sharding import PartitionSpec as P

BLOCK = 128
ITERS = 2
SCORE_GAIN = 0.0875
LOG2E = 1.4426950408889634
OFF = 1e30
DEPTH = 208

VMEM = pl.BlockSpec(memory_space=pltpu.VMEM)
SMEM = pl.BlockSpec(memory_space=pltpu.SMEM)
PARAMS = pltpu.CompilerParams(vmem_limit_bytes=48 * 1024 * 1024)


def pieces(x):
    first = x.astype(jnp.bfloat16).astype(jnp.float32)
    rest = x - first
    second = rest.astype(jnp.bfloat16).astype(jnp.float32)
    third = (rest - second).astype(jnp.bfloat16).astype(jnp.float32)
    return first, second, third


def allowance_of(spend_class, ratio):
    return ratio * jnp.exp(0.3 * spend_class.astype(jnp.float32) - 1.2)


def prepare_kernel(ratio, imps, elig_ref, class_ref, scale_ref, imp_ref, pack_ref, extra_ref):
    spend_class = class_ref[...].astype(jnp.float32)
    allowance = allowance_of(class_ref[...], ratio) / imps
    log_scale = jnp.log(scale_ref[...]) * LOG2E + ((0.3 * spend_class - 1.2) * LOG2E + math.log2(ratio / imps))
    parts = pieces(log_scale)
    rows, cols = class_ref.shape[0], elig_ref.shape[0]
    width = imp_ref.shape[1]
    pack_ref[0:64, :] = imp_ref[...]
    ones = jnp.ones((1, BLOCK), jnp.float32)
    sums = [jnp.zeros((1, BLOCK), jnp.float32) for _ in range(cols)]
    for b in range(rows):
        masks = []
        for c in range(cols):
            flag = elig_ref[c, b].astype(jnp.float32)
            sums[c] = sums[c] + flag * allowance[b : b + 1]
            masks.append(ones * ((flag - 1.0) * OFF))
        block = masks + [p[b : b + 1] for p in parts] + [ones] * 3
        block += [jnp.zeros((16 - len(block), BLOCK), jnp.float32)]
        extra_ref[:, b * BLOCK : (b + 1) * BLOCK] = jnp.concatenate(block, axis=0)
    totals = jnp.concatenate(
        [jnp.broadcast_to(jnp.sum(s, axis=1, keepdims=True), (1, BLOCK)) for s in sums], axis=1
    )
    pack_ref[64:72, :] = jnp.zeros((8, width), jnp.float32)
    for r in range(cols * BLOCK // width):
        pack_ref[64 + r : 65 + r, :] = totals[:, r * width : (r + 1) * width]


def first_kernel(groups, cols, place_ref, *refs):
    adv_refs = refs[:groups]
    own_ref, other_ref, extra_ref, gain_ref, sums_ref, price_ref, rhs_ref, lhs_ref, step_ref = refs[groups:]
    order, half = place_ref[0], place_ref[1]
    width = own_ref.shape[1]
    count = cols * BLOCK
    for ref, at in ((own_ref, half * width), (other_ref, (1 - half) * width)):
        block = ref[0:64, :] * (SCORE_GAIN * LOG2E)
        high = block.astype(jnp.bfloat16)
        low = (block - high.astype(jnp.float32)).astype(jnp.bfloat16)
        at = pl.multiple_of(at, width)
        lhs_ref[0:64, pl.ds(at, width)] = high
        lhs_ref[64:128, pl.ds(at, width)] = low
        lhs_ref[128:192, pl.ds(at, width)] = high
    price_parts = own_ref[64:72, :] + other_ref[64:72, :]
    price = jnp.concatenate([price_parts[r : r + 1] for r in range(count // width)], axis=1)
    column = lax.broadcasted_iota(jnp.int32, (1, count), 1) // BLOCK
    rows = [(column == c).astype(jnp.float32) for c in range(cols)]
    rows += [jnp.ones((1, count), jnp.float32)] * 3
    rows += list(pieces(-jnp.log(price) * LOG2E))
    rows += [jnp.zeros((16 - len(rows), count), jnp.float32)]
    lhs_ref[192:208, :] = jnp.concatenate(rows, axis=0).astype(jnp.bfloat16)
    for c in range(cols):
        price_ref[c : c + 1, :] = price[:, c * BLOCK : (c + 1) * BLOCK]
    lhs = lhs_ref[...].T
    k = 0
    for ref in adv_refs:
        for p in range(ref.shape[0]):
            lanes = slice(k * BLOCK, (k + 1) * BLOCK)
            b = order ^ k
            block = ref[p]
            high = block.astype(jnp.bfloat16)
            low = (block - high.astype(jnp.float32)).astype(jnp.bfloat16)
            rhs_ref[0:64, lanes] = high
            rhs_ref[64:128, lanes] = high
            rhs_ref[128:192, lanes] = low
            rhs_ref[192:208, lanes] = extra_ref[:, pl.ds(pl.multiple_of(b * BLOCK, BLOCK), BLOCK)].astype(jnp.bfloat16)
            k += 1
            if k % 2 == 0:
                two = slice((k - 2) * BLOCK, k * BLOCK)
                gain = jnp.exp2(jnp.dot(lhs, rhs_ref[:, two], preferred_element_type=jnp.float32))
                gain_ref[:, two] = gain
                sums = jnp.sum(gain, axis=0, keepdims=True)
                sums_ref[pl.ds(order ^ (k - 2), 1), :] = sums[:, :BLOCK]
                sums_ref[pl.ds(order ^ (k - 1), 1), :] = sums[:, BLOCK:]


def prices_kernel(ratio, place_ref, gain_ref, class_ref, *refs):
    *sum_refs, part_ref, pacing_ref = refs
    order = place_ref[0]
    allowance = allowance_of(class_ref[...], ratio)
    pacing_ref[...] = allowance / jnp.maximum(tree([r[...] for r in sum_refs]), allowance)
    blocks = class_ref.shape[0]
    for c in range(gain_ref.shape[0] // BLOCK):
        total = jnp.zeros((BLOCK, BLOCK), jnp.float32)
        for k in range(blocks):
            gain = gain_ref[c * BLOCK : (c + 1) * BLOCK, k * BLOCK : (k + 1) * BLOCK]
            total = total + gain * pacing_ref[pl.ds(order ^ k, 1), :]
        part_ref[c : c + 1, :] = jnp.sum(total.T, axis=0, keepdims=True)


def second_kernel(ratio, imps, place_ref, gain_ref, class_ref, pacing_ref, price_ref, *refs):
    *part_refs, next_ref, sums_ref, prices_ref, factor_ref, step_ref = refs
    order = place_ref[0]
    prices = tree([r[...] for r in part_refs])
    prices_ref[...] = prices
    ratio_rows = price_ref[...] / prices
    factor_ref[...] = pacing_ref[...] * (imps / allowance_of(class_ref[...], ratio))
    blocks = class_ref.shape[0]
    count = gain_ref.shape[0]
    for c in range(count // BLOCK):
        step_ref[c * BLOCK : (c + 1) * BLOCK, :] = jnp.broadcast_to(ratio_rows[c : c + 1], (BLOCK, BLOCK)).T
    for k in range(blocks):
        lanes = slice(k * BLOCK, (k + 1) * BLOCK)
        factor = factor_ref[pl.ds(order ^ k, 1), :]
        total = jnp.zeros((8, BLOCK), jnp.float32)
        for c in range(count // BLOCK):
            rows = slice(c * BLOCK, (c + 1) * BLOCK)
            gain = gain_ref[rows, lanes]
            new = (gain * factor) * (gain * step_ref[rows, :])
            next_ref[rows, lanes] = new
            total = total + jnp.sum(new.reshape(BLOCK // 8, 8, BLOCK), axis=0)
        sums_ref[pl.ds(order ^ k, 1), :] = jnp.sum(total, axis=0, keepdims=True)


def final_kernel(ratio, advs, per_step, place_ref, gain_ref, class_ref, *refs):
    *sum_refs, out_ref, pacing_ref, factor_ref = refs
    order = place_ref[0]
    step = pl.program_id(0)

    @pl.when(step == 0)
    def _():
        allowance = allowance_of(class_ref[...], ratio)
        pacing = allowance / jnp.maximum(tree([r[...] for r in sum_refs]), allowance)
        pacing_ref[...] = pacing
        factor_ref[...] = pacing * advs

    for p in range(per_step):
        b = step * per_step + p
        factor = factor_ref[pl.ds(b, 1), :]
        lanes = pl.ds(pl.multiple_of((b ^ order) * BLOCK, BLOCK), BLOCK)
        for c in range(gain_ref.shape[0] // BLOCK):
            block = gain_ref[c * BLOCK : (c + 1) * BLOCK, lanes] * factor
            out_ref[p * BLOCK : (p + 1) * BLOCK, c * BLOCK : (c + 1) * BLOCK] = block.T


def tree(terms):
    while len(terms) > 1:
        terms = [a + b for a, b in zip(terms[::2], terms[1::2])]
    return terms[0]


def swap(x, axis, k):
    return lax.ppermute(x, axis, [(i, i ^ k) for i in range(lax.axis_size(axis))])


def with_partners(x, axis, keys):
    return [x] + [swap(x, axis, k) for k in keys]


def stages(n):
    found, bit = [], 1
    while bit < n:
        found.append((bit, 2 * bit, 3 * bit) if 4 * bit <= n else (bit,))
        bit *= 4
    return found


def terms_of_sum(x, axis):
    n = lax.axis_size(axis)
    if n & (n - 1):
        return [lax.psum(x, axis)]
    todo = stages(n)
    for keys in todo[:-1]:
        x = tree(with_partners(x, axis, keys))
    return with_partners(x, axis, todo[-1])


def per_device(adv_embed, imp_embed, value_scale, spend_class, eligible):
    n_adv, n_imp = lax.axis_size("adv"), lax.axis_size("imp")
    adv_count = spend_class.shape[0]
    rows, cols = eligible.shape
    imp_count = cols * BLOCK
    imps, advs = imp_count * n_imp, adv_count * n_adv
    ratio = imps / advs
    f32 = jnp.float32
    class_rows = spend_class.reshape(rows, BLOCK)
    scale_rows = value_scale.reshape(rows, BLOCK)

    def shape(*dims):
        return jax.ShapeDtypeStruct(dims, f32)

    staged = n_imp == 16 and adv_embed.shape[0] == BLOCK and n_adv == 2
    imp_t = imp_embed.T
    if not staged:
        imp_t = lax.all_gather(imp_embed, "adv", axis=0, tiled=True).T[:, : imp_count // 2]
    width = imp_t.shape[1]
    pack, extra = pl.pallas_call(
        lambda *refs: prepare_kernel(ratio, imps, *refs),
        out_shape=(shape(72, width), shape(16, adv_count)),
        in_specs=[SMEM, VMEM, VMEM, VMEM],
        out_specs=(VMEM, VMEM),
        compiler_params=PARAMS,
    )(eligible.T, class_rows, scale_rows, imp_t)
    if staged:
        me, half = lax.axis_index("imp"), lax.axis_index("adv")
        line = jnp.stack(with_partners(adv_embed.T, "imp", (4, 8, 12)))
        other = swap(pack, "adv", 1)
        line, other = lax.optimization_barrier((line, other))
        plane = jnp.stack([line, swap(line, "imp", 2)], axis=1)
        pair = swap(plane, "imp", 1)
        adv_blocks = [jnp.stack([plane, pair], axis=2).reshape(rows, 64, BLOCK)]
    else:
        me, half = jnp.int32(0), jnp.int32(0)
        gathered = lax.all_gather(adv_embed, "imp", axis=0, tiled=True)
        adv_blocks = [gathered.reshape(rows, BLOCK, 64).transpose(0, 2, 1)]
        whole = lax.all_gather(imp_embed, "adv", axis=0, tiled=True).T[:, imp_count // 2 :]
        price = lax.psum(pack[64:], "adv")
        other = jnp.concatenate([whole, jnp.zeros_like(price)])
        pack = jnp.concatenate([pack[:64], price])
    place = jnp.stack([me, half]).astype(jnp.int32)

    gain, sums, first_price = pl.pallas_call(
        lambda *refs: first_kernel(len(adv_blocks), cols, *refs),
        out_shape=(pltpu.VMEM((imp_count, adv_count), f32), shape(rows, BLOCK), shape(cols, BLOCK)),
        in_specs=[SMEM] + [VMEM] * (len(adv_blocks) + 3),
        out_specs=(VMEM, VMEM, VMEM),
        scratch_shapes=[
            pltpu.VMEM((DEPTH, adv_count), jnp.bfloat16),
            pltpu.VMEM((DEPTH, imp_count), jnp.bfloat16),
            pltpu.VMEM((8, BLOCK), f32),
        ],
        compiler_params=PARAMS,
    )(place, *adv_blocks, pack, other, extra)

    terms = terms_of_sum(sums, "imp")
    part, pacing = pl.pallas_call(
        lambda *refs: prices_kernel(ratio, *refs),
        out_shape=(shape(cols, BLOCK), shape(rows, BLOCK)),
        in_specs=[SMEM] + [VMEM] * (2 + len(terms)),
        out_specs=(VMEM, VMEM),
        compiler_params=PARAMS,
    )(place, gain, class_rows, *terms)

    terms = terms_of_sum(part, "adv")
    gain, sums, prices = pl.pallas_call(
        lambda *refs: second_kernel(ratio, imps, *refs),
        out_shape=(pltpu.VMEM((imp_count, adv_count), f32), shape(rows, BLOCK), shape(cols, BLOCK)),
        in_specs=[SMEM] + [VMEM] * (4 + len(terms)),
        out_specs=(VMEM, VMEM, VMEM),
        scratch_shapes=[pltpu.VMEM((rows, BLOCK), f32), pltpu.VMEM((imp_count, BLOCK), f32)],
        input_output_aliases={1: 0},
        compiler_params=PARAMS,
    )(place, gain, class_rows, pacing, first_price, *terms)

    terms = terms_of_sum(sums, "imp")
    per_step = 2
    density, pacing = pl.pallas_call(
        lambda *refs: final_kernel(ratio, advs, per_step, *refs),
        grid=(rows // per_step,),
        out_shape=(shape(adv_count, imp_count), shape(rows, BLOCK)),
        in_specs=[SMEM] + [VMEM] * (2 + len(terms)),
        out_specs=(pl.BlockSpec((per_step * BLOCK, imp_count), lambda i: (i, 0)), VMEM),
        scratch_shapes=[pltpu.VMEM((rows, BLOCK), f32)],
        compiler_params=PARAMS,
    )(place, gain, class_rows, *terms)
    return density, prices.reshape(imp_count), pacing.reshape(adv_count)


def solution(mesh):
    in_specs = (
        P(("adv", "imp"), None),
        P(("imp", "adv"), None),
        P("adv"),
        P("adv"),
        P("adv", "imp"),
    )
    out_specs = (P("adv", "imp"), P("imp"), P("adv"))
    return jax.shard_map(
        per_device, mesh=mesh, in_specs=in_specs, out_specs=out_specs, check_vma=False
    )
```

```python
import math

import jax
import jax.numpy as jnp
from jax import lax
from jax.experimental import pallas as pl
from jax.experimental.pallas import tpu as pltpu
from jax.sharding import PartitionSpec as P

BLOCK = 128
ITERS = 2
SCORE_GAIN = 0.0875
LOG2E = 1.4426950408889634
OFF = 1e30
DEPTH = 208

VMEM = pl.BlockSpec(memory_space=pltpu.VMEM)
HBM = pl.BlockSpec(memory_space=pltpu.HBM)
PARAMS = pltpu.CompilerParams(vmem_limit_bytes=48 * 1024 * 1024)


def pieces(x):
    first = x.astype(jnp.bfloat16).astype(jnp.float32)
    rest = x - first
    second = rest.astype(jnp.bfloat16).astype(jnp.float32)
    third = (rest - second).astype(jnp.bfloat16).astype(jnp.float32)
    return first, second, third


def place(axis, staged):
    return lax.axis_index(axis) if staged else jnp.int32(0)


def prepare_kernel(ratio, imps, elig_hbm, class_hbm, scale_hbm, imp_hbm, adv_hbm, pack_ref, extra_ref, limit_ref, own_ref, elig_ref, class_ref, scale_ref, sems):
    moves = ((elig_hbm, elig_ref), (class_hbm, class_ref), (scale_hbm, scale_ref), (imp_hbm, pack_ref.at[0:64]), (adv_hbm, own_ref))
    copies = [pltpu.make_async_copy(src, dst, sems.at[n]) for n, (src, dst) in enumerate(moves)]
    for copy in copies:
        copy.start()
    for copy in copies:
        copy.wait()
    spend_class = class_ref[...].astype(jnp.float32)
    limit_ref[...] = ratio * jnp.exp(0.3 * spend_class - 1.2)
    allowance = limit_ref[...] / imps
    log_scale = jnp.log(scale_ref[...]) * LOG2E + ((0.3 * spend_class - 1.2) * LOG2E + math.log2(ratio / imps))
    parts = pieces(log_scale)
    rows, cols = class_ref.shape[0], elig_ref.shape[0]
    width = pack_ref.shape[1]
    ones = jnp.ones((1, BLOCK), jnp.float32)
    sums = [jnp.zeros((1, BLOCK), jnp.float32) for _ in range(cols)]
    for b in range(rows):
        masks = []
        for c in range(cols):
            flag = elig_ref[c : c + 1, b : b + 1].astype(jnp.float32)
            sums[c] = sums[c] + flag * allowance[b : b + 1]
            masks.append(ones * ((flag - 1.0) * OFF))
        block = masks + [p[b : b + 1] for p in parts] + [ones] * 3
        block += [jnp.zeros((16 - len(block), BLOCK), jnp.float32)]
        extra_ref[:, b * BLOCK : (b + 1) * BLOCK] = jnp.concatenate(block, axis=0).astype(jnp.bfloat16)
    totals = jnp.concatenate(
        [jnp.broadcast_to(jnp.sum(s, axis=1, keepdims=True), (1, BLOCK)) for s in sums], axis=1
    )
    pack_ref[64:72, :] = jnp.zeros((8, width), jnp.float32)
    for r in range(cols * BLOCK // width):
        pack_ref[64 + r : 65 + r, :] = totals[:, r * width : (r + 1) * width]


def impressions_kernel(staged, cols, own_ref, other_ref, lhs_ref, lhs_t_ref, price_ref):
    half = place("adv", staged)
    width = own_ref.shape[1]
    count = cols * BLOCK
    for ref, at in ((own_ref, half * width), (other_ref, (1 - half) * width)):
        block = ref[0:64, :] * (SCORE_GAIN * LOG2E)
        high = block.astype(jnp.bfloat16)
        low = (block - high.astype(jnp.float32)).astype(jnp.bfloat16)
        at = pl.multiple_of(at, width)
        lhs_ref[0:64, pl.ds(at, width)] = high
        lhs_ref[64:128, pl.ds(at, width)] = low
        lhs_ref[128:192, pl.ds(at, width)] = high
    price_parts = own_ref[64:72, :] + other_ref[64:72, :]
    price = jnp.concatenate([price_parts[r : r + 1] for r in range(count // width)], axis=1)
    column = lax.broadcasted_iota(jnp.int32, (1, count), 1) // BLOCK
    rows = [(column == c).astype(jnp.float32) for c in range(cols)]
    rows += [jnp.ones((1, count), jnp.float32)] * 3
    rows += list(pieces(-jnp.log(price) * LOG2E))
    rows += [jnp.zeros((16 - len(rows), count), jnp.float32)]
    lhs_ref[192:208, :] = jnp.concatenate(rows, axis=0).astype(jnp.bfloat16)
    for c in range(cols):
        price_ref[c : c + 1, :] = price[:, c * BLOCK : (c + 1) * BLOCK]
    lhs_t_ref[...] = lhs_ref[...].T


def first_kernel(staged, keys, adv_ref, extra_ref, lhs_t_ref, *refs):
    gain_ref, sums_ref, rhs_ref = refs[-3:]
    order = place("imp", staged)
    lhs = lhs_t_ref[...]
    for n in range(0, len(keys), 2):
        two = keys[n : n + 2]
        for p, k in enumerate(two):
            lanes = slice(k * BLOCK, (k + 1) * BLOCK)
            block = adv_ref[n + p]
            high = block.astype(jnp.bfloat16)
            low = (block - high.astype(jnp.float32)).astype(jnp.bfloat16)
            rhs_ref[0:64, lanes] = high
            rhs_ref[64:128, lanes] = high
            rhs_ref[128:192, lanes] = low
            at = pl.multiple_of((order ^ k) * BLOCK, BLOCK)
            rhs_ref[192:208, lanes] = extra_ref[:, pl.ds(at, BLOCK)]
        rhs = jnp.concatenate([rhs_ref[:, k * BLOCK : (k + 1) * BLOCK] for k in two], axis=1)
        gain = jnp.exp2(jnp.dot(lhs, rhs, preferred_element_type=jnp.float32))
        sums = jnp.sum(gain, axis=0, keepdims=True)
        for p, k in enumerate(two):
            gain_ref[:, k * BLOCK : (k + 1) * BLOCK] = gain[:, p * BLOCK : (p + 1) * BLOCK]
            sums_ref[pl.ds(order ^ k, 1), :] = sums[:, p * BLOCK : (p + 1) * BLOCK]


def rows_kernel(lhs_ref, rhs_ref, gain_ref):
    lhs = lhs_ref[...]
    for k in range(rhs_ref.shape[1] // BLOCK):
        rows = slice(k * BLOCK, (k + 1) * BLOCK)
        gain_ref[rows, :] = jnp.exp2(jnp.dot(rhs_ref[:, rows].T, lhs, preferred_element_type=jnp.float32))


def prices_kernel(staged, gain_ref, limit_ref, *refs):
    *sum_refs, part_ref, pacing_ref = refs
    order = place("imp", staged)
    limit = limit_ref[...]
    pacing_ref[...] = limit / jnp.maximum(tree([r[...] for r in sum_refs]), limit)
    factors = [pacing_ref[pl.ds(order ^ k, 1), :] for k in range(limit.shape[0])]
    for c in range(gain_ref.shape[0] // BLOCK):
        total = jnp.zeros((BLOCK, BLOCK), jnp.float32)
        for k, factor in enumerate(factors):
            total = total + gain_ref[c * BLOCK : (c + 1) * BLOCK, k * BLOCK : (k + 1) * BLOCK] * factor
        part_ref[c : c + 1, :] = jnp.sum(total.T, axis=0, keepdims=True)


def second_kernel(staged, imps, gain_ref, limit_ref, pacing_ref, price_ref, *refs):
    *part_refs, sums_ref, prices_ref, factor_ref, change_ref = refs
    order = place("imp", staged)
    prices = tree([r[...] for r in part_refs])
    prices_ref[...] = prices
    changes = price_ref[...] / prices
    factor_ref[...] = pacing_ref[...] * (imps / limit_ref[...])
    blocks = limit_ref.shape[0]
    factors = [factor_ref[pl.ds(order ^ k, 1), :] for k in range(blocks)]
    totals = [jnp.zeros((8, BLOCK), jnp.float32) for _ in range(blocks)]
    for c in range(gain_ref.shape[0] // BLOCK):
        change_ref[:, c * BLOCK : (c + 1) * BLOCK] = changes[c : c + 1]
        change = jnp.broadcast_to(changes[c : c + 1], (BLOCK, BLOCK)).T
        for k in range(blocks):
            gain = gain_ref[c * BLOCK : (c + 1) * BLOCK, k * BLOCK : (k + 1) * BLOCK]
            new = (gain * factors[k]) * (gain * change)
            totals[k] = totals[k] + jnp.sum(new.reshape(BLOCK // 8, 8, BLOCK), axis=0)
    for k in range(blocks):
        sums_ref[pl.ds(order ^ k, 1), :] = jnp.sum(totals[k], axis=0, keepdims=True)


def final_kernel(staged, advs, gain_ref, limit_ref, factor_ref, change_ref, *refs):
    *sum_refs, out_ref, pacing_ref, scale_ref, block_ref, sems = refs
    order = place("imp", staged)
    limit = limit_ref[...]
    pacing = limit / jnp.maximum(tree([r[...] for r in sum_refs]), limit)
    pacing_ref[...] = pacing
    scale_ref[...] = pacing * factor_ref[...] * advs
    change = change_ref[...]
    shape = (BLOCK, BLOCK)
    diagonal = lax.broadcasted_iota(jnp.int32, shape, 0) == lax.broadcasted_iota(jnp.int32, shape, 1)
    copies = []
    for k in range(limit.shape[0]):
        b = order ^ k
        rows = slice(k * BLOCK, (k + 1) * BLOCK)
        scale = jnp.sum(jnp.where(diagonal, scale_ref[pl.ds(b, 1), :], 0.0), axis=1, keepdims=True)
        gain = gain_ref[rows, :]
        block_ref[rows, :] = (gain * scale) * (gain * change)
        to = pl.ds(pl.multiple_of(b * BLOCK, BLOCK), BLOCK)
        copy = pltpu.make_async_copy(block_ref.at[rows], out_ref.at[to], sems.at[k])
        copy.start()
        copies.append(copy)
    for copy in copies:
        copy.wait()


def tree(terms):
    while len(terms) > 1:
        terms = [a + b for a, b in zip(terms[::2], terms[1::2])]
    return terms[0]


def swap(x, axis, k):
    return lax.ppermute(x, axis, [(i, i ^ k) for i in range(lax.axis_size(axis))])


def with_partners(x, axis, keys):
    return [x] + [swap(x, axis, k) for k in keys]


def stages(n):
    found, bit = [], 1
    while bit < n:
        found.append((bit, 2 * bit, 3 * bit) if 4 * bit <= n else (bit,))
        bit *= 4
    return found


def terms_of_sum(x, axis):
    n = lax.axis_size(axis)
    if n & (n - 1):
        return [lax.psum(x, axis)]
    todo = stages(n)
    for keys in todo[:-1]:
        x = tree(with_partners(x, axis, keys))
    return with_partners(x, axis, todo[-1])


def per_device(adv_embed, imp_embed, value_scale, spend_class, eligible):
    n_adv, n_imp = lax.axis_size("adv"), lax.axis_size("imp")
    adv_count = spend_class.shape[0]
    rows, cols = eligible.shape
    imp_count = cols * BLOCK
    imps, advs = imp_count * n_imp, adv_count * n_adv
    ratio = imps / advs
    f32 = jnp.float32
    class_rows = spend_class.reshape(rows, BLOCK)
    scale_rows = value_scale.reshape(rows, BLOCK)

    def shape(*dims, dtype=f32):
        return jax.ShapeDtypeStruct(dims, dtype)

    def call(kernel, out, operands, cost=0, **kw):
        return pl.pallas_call(
            kernel,
            out_shape=out,
            in_specs=[VMEM] * len(operands),
            out_specs=tuple(VMEM for _ in out),
            compiler_params=PARAMS,
            cost_estimate=pl.CostEstimate(flops=cost, bytes_accessed=cost // 256, transcendentals=0),
            **kw,
        )(*operands)

    staged = n_imp == 16 and adv_embed.shape[0] == BLOCK and n_adv == 2
    imp_t, adv_t = imp_embed.T, adv_embed.T
    if not staged:
        imp_t = lax.all_gather(imp_embed, "adv", axis=0, tiled=True).T[:, : imp_count // 2]
    width = imp_t.shape[1]
    ins = [pltpu.with_memory_space_constraint(x, pltpu.HBM) for x in (eligible.T, class_rows, scale_rows, imp_t, adv_t)]
    pack, extra, limit, own = pl.pallas_call(
        lambda *refs: prepare_kernel(ratio, imps, *refs),
        out_shape=(shape(72, width), shape(16, adv_count, dtype=jnp.bfloat16), shape(rows, BLOCK), shape(*adv_t.shape)),
        in_specs=[HBM] * len(ins),
        out_specs=(VMEM,) * 4,
        scratch_shapes=[
            pltpu.VMEM((cols, rows), jnp.int32),
            pltpu.VMEM((rows, BLOCK), jnp.int32),
            pltpu.VMEM((rows, BLOCK), f32),
            pltpu.SemaphoreType.DMA((len(ins),)),
        ],
        compiler_params=PARAMS,
    )(*ins)
    if staged:
        line = jnp.stack([own] + [swap(adv_t, "imp", k) for k in (4, 8, 12)])
        other = swap(pack, "adv", 1)
        plane = swap(line, "imp", 2)
        plane, _ = lax.optimization_barrier((plane, other))
        pair = swap(jnp.concatenate([line, plane]), "imp", 1)
        groups = [((0, 4, 8, 12), line), ((2, 6, 10, 14), plane), ((1, 5, 9, 13, 3, 7, 11, 15), pair)]
    else:
        gathered = lax.all_gather(adv_embed, "imp", axis=0, tiled=True)
        groups = [(tuple(range(rows)), gathered.reshape(rows, BLOCK, 64).transpose(0, 2, 1))]
        whole = lax.all_gather(imp_embed, "adv", axis=0, tiled=True).T[:, imp_count // 2 :]
        price = lax.psum(pack[64:], "adv")
        other = jnp.concatenate([whole, jnp.zeros_like(price)])
        pack = jnp.concatenate([pack[:64], price])

    bf16 = jnp.bfloat16
    lhs, lhs_t, first_price = call(
        lambda *refs: impressions_kernel(staged, cols, *refs),
        (shape(DEPTH, imp_count, dtype=bf16), shape(imp_count, DEPTH, dtype=bf16), shape(cols, BLOCK)),
        (pack, other),
        cost=10**8,
    )
    held = ()
    for keys, blocks in groups:
        held = call(
            lambda *refs, keys=keys: first_kernel(staged, keys, *refs),
            (
                pltpu.VMEM((imp_count, adv_count), f32),
                shape(rows, BLOCK),
                pltpu.VMEM((DEPTH, adv_count), bf16),
            ),
            (blocks, extra, lhs_t, *held),
            cost=10**8 * len(keys),
            input_output_aliases={3 + i: i for i in range(len(held))},
        )
    gain, sums, rhs = held
    (gain_rows,) = call(rows_kernel, (pltpu.VMEM((adv_count, imp_count), f32),), (lhs, rhs), cost=10**9)

    part, pacing = call(
        lambda *refs: prices_kernel(staged, *refs), (shape(cols, BLOCK), shape(rows, BLOCK)), (gain, limit, *terms_of_sum(sums, "imp"))
    )
    sums, prices, factor, change = call(
        lambda *refs: second_kernel(staged, imps, *refs),
        (shape(rows, BLOCK), shape(cols, BLOCK), shape(rows, BLOCK), shape(1, imp_count)),
        (gain, limit, pacing, first_price, *terms_of_sum(part, "adv")),
    )

    terms = terms_of_sum(sums, "imp")
    density, pacing = pl.pallas_call(
        lambda *refs: final_kernel(staged, advs, *refs),
        out_shape=(shape(adv_count, imp_count), shape(rows, BLOCK)),
        in_specs=[VMEM] * (4 + len(terms)),
        out_specs=(HBM, VMEM),
        scratch_shapes=[
            pltpu.VMEM((rows, BLOCK), f32),
            pltpu.VMEM((adv_count, imp_count), f32),
            pltpu.SemaphoreType.DMA((rows,)),
        ],
        compiler_params=PARAMS,
    )(gain_rows, limit, factor, change, *terms)
    return density, prices.reshape(imp_count), pacing.reshape(adv_count)


def solution(mesh):
    in_specs = (
        P(("adv", "imp"), None),
        P(("imp", "adv"), None),
        P("adv"),
        P("adv"),
        P("adv", "imp"),
    )
    out_specs = (P("adv", "imp"), P("imp"), P("adv"))
    return jax.shard_map(
        per_device, mesh=mesh, in_specs=in_specs, out_specs=out_specs, check_vma=False
    )
```

```python
import math

import jax
import jax.numpy as jnp
from jax import lax
from jax.experimental import pallas as pl
from jax.experimental.pallas import tpu as pltpu
from jax.sharding import PartitionSpec as P

BLOCK = 128
ITERS = 2
SCORE_GAIN = 0.0875
LOG2E = 1.4426950408889634
OFF = 1e30
EMB = 64
DEPTH = 3 * EMB + 16
F32, BF16 = jnp.float32, jnp.bfloat16

VMEM = pl.BlockSpec(memory_space=pltpu.VMEM)
HBM = pl.BlockSpec(memory_space=pltpu.HBM)
PARAMS = pltpu.CompilerParams(vmem_limit_bytes=16 * 1024 * 1024)


def home():
    m = lax.axis_index("imp")
    return m, (m >> 2) & 1


def pieces(x):
    first = x.astype(BF16).astype(F32)
    rest = x - first
    second = rest.astype(BF16).astype(F32)
    third = (rest - second).astype(BF16).astype(F32)
    return first, second, third


def halves(block):
    high = block.astype(BF16)
    return high, (block - high.astype(F32)).astype(BF16)


def tree(terms):
    while len(terms) > 1:
        terms = [a + b for a, b in zip(terms[::2], terms[1::2])]
    return terms[0]


def in_order(w, own, other):
    return jnp.concatenate([jnp.where(w == 0, own, other), jnp.where(w == 0, other, own)], axis=0)


def prepare_kernel(
    ratio, imps, elig_hbm, class_hbm, scale_hbm, imp_hbm, adv_hbm,
    pack_ref, logs_ref, limit_ref, own_ref, elig_ref, class_ref, scale_ref, sems,
):
    moves = (
        (elig_hbm, elig_ref),
        (class_hbm, class_ref),
        (scale_hbm, scale_ref),
        (imp_hbm, pack_ref.at[0:EMB]),
        (adv_hbm, own_ref),
    )
    copies = [pltpu.make_async_copy(src, dst, sems.at[n]) for n, (src, dst) in enumerate(moves)]
    for copy in copies:
        copy.start()
    for copy in copies:
        copy.wait()
    exponent = 0.3 * class_ref[...].astype(F32) - 1.2
    limit = ratio * jnp.exp(exponent)
    limit_ref[...] = limit
    logs_ref[...] = jnp.log(scale_ref[...]) * LOG2E + (exponent * LOG2E + math.log2(ratio / imps))
    rows, cols = class_ref.shape[0], elig_ref.shape[0]
    flags = elig_ref[...].astype(F32)
    allowance = limit / imps
    totals = []
    for c in range(cols):
        total = jnp.zeros((1, BLOCK), F32)
        for b in range(rows):
            total = total + flags[c : c + 1, b : b + 1] * allowance[b : b + 1]
        totals.append(jnp.broadcast_to(jnp.sum(total, axis=1, keepdims=True), (1, BLOCK)))
    pack_ref[EMB : EMB + 8, :] = jnp.zeros((8, pack_ref.shape[1]), F32)
    for c in range(cols):
        pack_ref[EMB + c // 2 : EMB + c // 2 + 1, c % 2 * BLOCK : (c % 2 + 1) * BLOCK] = totals[c]
    pack_ref[EMB + 4 : EMB + 4 + cols, 0:rows] = flags


def own_flags(pack_ref, cols, rows):
    return pack_ref[EMB + 4 : EMB + 4 + cols, 0:rows]


def extra_rows(flags, logs):
    cols, rows = flags.shape
    count = logs.shape[0] * BLOCK
    at = lax.broadcasted_iota(jnp.int32, (rows, count), 0)
    spread = (at == lax.broadcasted_iota(jnp.int32, (rows, count), 1) // BLOCK).astype(BF16)
    masks = (jnp.dot(flags.astype(BF16), spread, preferred_element_type=F32) - 1.0) * OFF
    line = jnp.concatenate([logs[r : r + 1] for r in range(logs.shape[0])], axis=1)
    ones = jnp.ones((1, count), F32)
    parts = [masks, *pieces(line), ones, ones, ones, jnp.zeros((10 - cols, count), F32)]
    return jnp.concatenate(parts, axis=0).astype(BF16)


def impressions_kernel(cols, rows, own_ref, down_ref, side_ref, cross_ref, logs_ref, lhs_ref, lhs_t_ref, extra_ref, price_ref):
    _, w = home()
    half = lax.axis_index("adv")
    width = own_ref.shape[1]
    count = 2 * cols * BLOCK
    places = ((own_ref, w, half), (down_ref, w, 1 - half), (side_ref, 1 - w, half), (cross_ref, 1 - w, 1 - half))
    for ref, side, part in places:
        high, low = halves(ref[0:EMB, :] * (SCORE_GAIN * LOG2E))
        at = pl.ds(pl.multiple_of(side * (2 * width) + part * width, width), width)
        lhs_ref[0:EMB, at] = high
        lhs_ref[EMB : 2 * EMB, at] = low
        lhs_ref[2 * EMB : 3 * EMB, at] = high
    rows_of = [a[EMB : EMB + 2, :] + b[EMB : EMB + 2, :] for a, b in ((own_ref, down_ref), (side_ref, cross_ref))]
    price = in_order(w, *rows_of)
    price = jnp.concatenate([price[r : r + 1] for r in range(4)], axis=1)
    column = lax.broadcasted_iota(jnp.int32, (2 * cols, count), 1) // BLOCK
    own = (column == lax.broadcasted_iota(jnp.int32, (2 * cols, count), 0)).astype(F32)
    ones = jnp.ones((1, count), F32)
    parts = [own, ones, ones, ones, *pieces(-jnp.log(price) * LOG2E), jnp.zeros((10 - 2 * cols, count), F32)]
    lhs_ref[3 * EMB :, :] = jnp.concatenate(parts, axis=0).astype(BF16)
    for c in range(2 * cols):
        price_ref[c : c + 1, :] = price[:, c * BLOCK : (c + 1) * BLOCK]
    lhs_t_ref[...] = lhs_ref[...].T
    flags = in_order(w, own_flags(own_ref, cols, rows), own_flags(side_ref, cols, rows))
    extra_ref[...] = extra_rows(flags, logs_ref[...])


def first_kernel(keys, adv_ref, extra_ref, lhs_t_ref, *refs):
    *earlier, gain_ref, sums_ref, rhs_ref = refs
    m, _ = home()
    count = gain_ref.shape[0]
    if earlier:
        sums_ref[...] = earlier[0][...]
    else:
        sums_ref[...] = jnp.zeros(sums_ref.shape, F32)
    for n in range(0, len(keys), 2):
        two = slice(n * BLOCK, (n + 2) * BLOCK)
        for p in range(2):
            lanes = slice((n + p) * BLOCK, (n + p + 1) * BLOCK)
            high, low = halves(adv_ref[n + p])
            rhs_ref[0:EMB, lanes] = high
            rhs_ref[EMB : 2 * EMB, lanes] = high
            rhs_ref[2 * EMB : 3 * EMB, lanes] = low
            at = pl.multiple_of((m ^ keys[n + p]) * BLOCK, BLOCK)
            rhs_ref[3 * EMB :, lanes] = extra_ref[:, pl.ds(at, BLOCK)]
        sums = jnp.zeros((1, 2 * BLOCK), F32)
        for h in range(2):
            part = slice(h * count // 2, (h + 1) * count // 2)
            gain = jnp.exp2(jnp.dot(lhs_t_ref[part, :], rhs_ref[:, two], preferred_element_type=F32))
            sums = sums + jnp.sum(gain, axis=0, keepdims=True)
            gain_ref[part, two] = gain
        for p in range(2):
            sums_ref[pl.ds(m ^ keys[n + p], 1), :] = sums[:, p * BLOCK : (p + 1) * BLOCK]


def rows_kernel(lhs_ref, *refs):
    *rhs_refs, gain_ref = refs
    _, w = home()
    width = gain_ref.shape[1]
    lhs = lhs_ref[:, pl.ds(pl.multiple_of(w * width, width), width)]
    at = 0
    for ref in rhs_refs:
        for lane in range(0, ref.shape[1], BLOCK):
            rhs = ref[:, lane : lane + BLOCK].T
            gain_ref[at : at + BLOCK, :] = jnp.exp2(jnp.dot(rhs, lhs, preferred_element_type=F32))
            at += BLOCK


def tiles(refs, c):
    rows = slice(c * BLOCK, (c + 1) * BLOCK)
    return [(ref, (rows, slice(lane, lane + BLOCK))) for ref in refs for lane in range(0, ref.shape[1], BLOCK)]


def prices_kernel(keys, parts, limit_ref, *refs):
    gains, sum_refs, (part_ref, pacing_ref), bids = refs[:parts], refs[parts : -2 - parts], refs[-2 - parts : -parts], refs[-parts:]
    m, _ = home()
    limit = limit_ref[...]
    pacing_ref[...] = limit / jnp.maximum(tree([ref[...] for ref in sum_refs]), limit)
    factors = [pacing_ref[pl.ds(m ^ k, 1), :] for k in keys]
    for c in range(part_ref.shape[0]):
        total = jnp.zeros((BLOCK, BLOCK), F32)
        for (gain_ref, at), (bid_ref, _), factor in zip(tiles(gains, c), tiles(bids, c), factors):
            bid = gain_ref[at] * factor
            bid_ref[at] = bid
            total = total + bid
        part_ref[c : c + 1, :] = jnp.sum(total.T, axis=0, keepdims=True)


def second_kernel(keys, parts, imps, limit_ref, pacing_ref, price_ref, *refs):
    bids, part_refs, (sums_ref, prices_ref, factor_ref, change_ref) = refs[:parts], refs[parts:-4], refs[-4:]
    m, w = home()
    prices = tree([ref[...] for ref in part_refs])
    changes = price_ref[...] / prices
    half = prices.shape[0] // 2
    prices_ref[...] = jnp.where(w == 0, prices[0:half], prices[half:])
    change = jnp.where(w == 0, changes[0:half], changes[half:])
    for c in range(half):
        change_ref[:, c * BLOCK : (c + 1) * BLOCK] = change[c : c + 1]
    factor_ref[...] = pacing_ref[...] * (imps / limit_ref[...])
    totals = [jnp.zeros((8, BLOCK), F32) for _ in keys]
    for c in range(2 * half):
        column = jnp.broadcast_to(changes[c : c + 1], (BLOCK, BLOCK)).T
        for n, (ref, at) in enumerate(tiles(bids, c)):
            bid = ref[at]
            totals[n] = totals[n] + jnp.sum((bid * (bid * column)).reshape(BLOCK // 8, 8, BLOCK), axis=0)
    for k, total in zip(keys, totals):
        sums_ref[pl.ds(m ^ k, 1), :] = jnp.sum(total, axis=0, keepdims=True)
    sums_ref[...] = sums_ref[...] * (imps / (limit_ref[...] * pacing_ref[...]))


def final_kernel(keys, advs, gain_ref, limit_ref, factor_ref, change_ref, *refs):
    *sum_refs, out_ref, pacing_out, pacing_ref, scale_ref, block_ref, sems = refs
    m, _ = home()
    limit = limit_ref[...]
    pacing = limit / jnp.maximum(tree([ref[...] for ref in sum_refs]), limit)
    scale_ref[...] = pacing * factor_ref[...] * advs
    pacing_ref[...] = pacing
    copies = [pltpu.make_async_copy(pacing_ref, pacing_out, sems.at[len(keys)])]
    copies[0].start()
    change = change_ref[...]
    shape = (BLOCK, BLOCK)
    diagonal = lax.broadcasted_iota(jnp.int32, shape, 0) == lax.broadcasted_iota(jnp.int32, shape, 1)
    for n, k in enumerate(keys):
        rows = slice(n * BLOCK, (n + 1) * BLOCK)
        scale = jnp.sum(jnp.where(diagonal, scale_ref[pl.ds(m ^ k, 1), :], 0.0), axis=1, keepdims=True)
        gain = gain_ref[rows, :]
        block_ref[rows, :] = (gain * scale) * (gain * change)
        to = pl.ds(pl.multiple_of((m ^ k) * BLOCK, BLOCK), BLOCK)
        copy = pltpu.make_async_copy(block_ref.at[rows], out_ref.at[to], sems.at[n])
        copy.start()
        copies.append(copy)
    for copy in copies:
        copy.wait()


def swap(x, axis, k):
    return lax.ppermute(x, axis, [(i, i ^ k) for i in range(lax.axis_size(axis))])


def with_partners(x, keys):
    return [x] + [swap(x, "imp", k) for k in keys]


def over_impressions(sums):
    return with_partners(tree(with_partners(sums, (1, 2, 3))), (8,))


def staged(adv_embed, imp_embed, value_scale, spend_class, eligible):
    adv_count = spend_class.shape[0]
    rows, cols = eligible.shape
    imp_count = cols * BLOCK
    imps, advs = imp_count * lax.axis_size("imp"), adv_count * lax.axis_size("adv")
    ratio = imps / advs

    def shape(*dims, dtype=F32):
        return jax.ShapeDtypeStruct(dims, dtype)

    def call(kernel, out, operands, cost=0, **kw):
        return pl.pallas_call(
            kernel,
            out_shape=out,
            in_specs=[VMEM] * len(operands),
            out_specs=tuple(VMEM for _ in out),
            compiler_params=PARAMS,
            cost_estimate=pl.CostEstimate(flops=cost, bytes_accessed=cost // 256, transcendentals=0),
            **kw,
        )(*operands)

    adv_t = adv_embed.T
    ins = (eligible.T, spend_class.reshape(rows, BLOCK), value_scale.reshape(rows, BLOCK), imp_embed.T, adv_t)
    ins = [pltpu.with_memory_space_constraint(x, pltpu.HBM) for x in ins]
    pack, logs, limit, own = pl.pallas_call(
        lambda *refs: prepare_kernel(ratio, imps, *refs),
        out_shape=(shape(EMB + 8, imp_embed.shape[0]), shape(rows, BLOCK), shape(rows, BLOCK), shape(*adv_t.shape)),
        in_specs=[HBM] * len(ins),
        out_specs=(VMEM,) * 4,
        scratch_shapes=[
            pltpu.VMEM((cols, rows), jnp.int32),
            pltpu.VMEM((rows, BLOCK), jnp.int32),
            pltpu.VMEM((rows, BLOCK), F32),
            pltpu.SemaphoreType.DMA((len(ins),)),
        ],
        compiler_params=PARAMS,
    )(*ins)
    line = jnp.stack([own, *with_partners(adv_t, (8, 12, 4))[1:]])
    down, side, cross = [swap(pack, ("adv", "imp"), k) for k in (16, 4, 20)]
    plane = swap(line, "imp", 2)
    plane, _ = lax.optimization_barrier((plane, (down, side, cross)))
    pair = swap(jnp.concatenate([line, plane]), "imp", 1)
    at_line = (0, 8, 12, 4)
    at_plane = tuple(k + 2 for k in at_line)
    at_pair = tuple(k + 1 for k in at_line + at_plane)
    keys = at_line + at_plane + at_pair

    count = 2 * imp_count
    lhs, lhs_t, extra, first_price = call(
        lambda *refs: impressions_kernel(cols, rows, *refs),
        (
            shape(DEPTH, count, dtype=BF16),
            shape(count, DEPTH, dtype=BF16),
            shape(16, adv_count, dtype=BF16),
            shape(2 * cols, BLOCK),
        ),
        (pack, down, side, cross, logs),
        cost=10**8,
    )
    gains, rhs, sums = [], [], ()
    for at, blocks in ((at_line, line), (at_plane, plane), (at_pair, pair)):
        width = len(at) * BLOCK
        gain, total, side = call(
            lambda *refs, at=at: first_kernel(at, *refs),
            (pltpu.VMEM((count, width), F32), shape(rows, BLOCK), pltpu.VMEM((DEPTH, width), BF16)),
            (blocks, extra, lhs_t, *sums),
            cost=10**8 * len(at),
        )
        gains.append(gain)
        rhs.append(side)
        sums = (total,)

    terms = over_impressions(sums[0])
    (gain_rows,) = call(rows_kernel, (pltpu.VMEM((adv_count, imp_count), F32),), (lhs, *rhs), cost=10**9)

    part, pacing, *bids = call(
        lambda *refs: prices_kernel(keys, len(gains), *refs),
        (shape(2 * cols, BLOCK), shape(rows, BLOCK), *(pltpu.VMEM(g.shape, F32) for g in gains)),
        (limit, *gains, *terms),
    )
    sums, prices, factor, change = call(
        lambda *refs: second_kernel(keys, len(gains), imps, *refs),
        (shape(rows, BLOCK), pltpu.VMEM((cols, BLOCK), F32), shape(rows, BLOCK), shape(1, imp_count)),
        (limit, pacing, first_price, *bids, part, swap(part, "adv", 1)),
    )

    terms = over_impressions(sums)
    density, pacing = pl.pallas_call(
        lambda *refs: final_kernel(keys, advs, *refs),
        out_shape=(shape(adv_count, imp_count), shape(rows, BLOCK)),
        in_specs=[VMEM] * (4 + len(terms)),
        out_specs=(HBM, HBM),
        scratch_shapes=[
            pltpu.VMEM((rows, BLOCK), F32),
            pltpu.VMEM((rows, BLOCK), F32),
            pltpu.VMEM((adv_count, imp_count), F32),
            pltpu.SemaphoreType.DMA((rows + 1,)),
        ],
        compiler_params=PARAMS,
    )(gain_rows, limit, factor, change, *terms)
    return density, prices.reshape(imp_count), pacing.reshape(adv_count)


def plain(adv_embed, imp_embed, value_scale, spend_class, eligible):
    imp_block = lax.all_gather(imp_embed, "adv", axis=0, tiled=True)
    rows = lax.all_gather(adv_embed, "imp", axis=0, tiled=True)
    scores = SCORE_GAIN * jnp.einsum(
        "ae,ie->ai", rows, imp_block, precision=lax.Precision.HIGHEST, preferred_element_type=F32
    )
    total_advs = scores.shape[0] * lax.axis_size("adv")
    total_imps = scores.shape[1] * lax.axis_size("imp")
    mask = jnp.repeat(jnp.repeat(eligible.astype(F32), BLOCK, axis=0), BLOCK, axis=1)
    values = value_scale[:, None] * jnp.exp(scores) * mask
    allowance = total_imps / total_advs * jnp.exp(0.3 * spend_class.astype(F32) - 1.2)
    bid_tile = mask * allowance[:, None] / total_imps
    for _ in range(ITERS):
        prices = lax.psum(jnp.sum(bid_tile, axis=0), "adv")
        gain = values * bid_tile / prices[None, :]
        spending = lax.psum(jnp.sum(gain, axis=1), "imp")
        pacing = allowance / jnp.maximum(spending, allowance)
        bid_tile = pacing[:, None] * gain
    return bid_tile * total_advs, prices, pacing


def per_device(adv_embed, imp_embed, value_scale, spend_class, eligible):
    sizes = (lax.axis_size("adv"), lax.axis_size("imp"), adv_embed.shape, imp_embed.shape, eligible.shape)
    fits = sizes == (2, 16, (BLOCK, EMB), (2 * BLOCK, EMB), (16, 4))
    return (staged if fits else plain)(adv_embed, imp_embed, value_scale, spend_class, eligible)


def solution(mesh):
    in_specs = (
        P(("adv", "imp"), None),
        P(("imp", "adv"), None),
        P("adv"),
        P("adv"),
        P("adv", "imp"),
    )
    out_specs = (P("adv", "imp"), P("imp"), P("adv"))
    return jax.shard_map(
        per_device, mesh=mesh, in_specs=in_specs, out_specs=out_specs, check_vma=False
    )
```

```python
import math

import jax
import jax.numpy as jnp
from jax import lax
from jax.experimental import pallas as pl
from jax.experimental.pallas import tpu as pltpu
from jax.sharding import PartitionSpec as P

BLOCK = 128
ITERS = 2
SCORE_GAIN = 0.0875
LOG2E = 1.4426950408889634
OFF = 1e30
EMB = 64
DEPTH = 3 * EMB + 16
F32, BF16 = jnp.float32, jnp.bfloat16

VMEM = pl.BlockSpec(memory_space=pltpu.VMEM)
HBM = pl.BlockSpec(memory_space=pltpu.HBM)
PARAMS = pltpu.CompilerParams(vmem_limit_bytes=16 * 1024 * 1024)


def home():
    m = lax.axis_index("imp")
    return m, (m >> 2) & 1


def pieces(x):
    first = x.astype(BF16).astype(F32)
    rest = x - first
    second = rest.astype(BF16).astype(F32)
    third = (rest - second).astype(BF16).astype(F32)
    return first, second, third


def halves(block):
    high = block.astype(BF16)
    return high, (block - high.astype(F32)).astype(BF16)


def tree(terms):
    while len(terms) > 1:
        terms = [a + b for a, b in zip(terms[::2], terms[1::2])]
    return terms[0]


def in_order(w, own, other):
    return jnp.concatenate([jnp.where(w == 0, own, other), jnp.where(w == 0, other, own)], axis=0)


def prepare_kernel(
    ratio, imps, elig_hbm, class_hbm, scale_hbm, imp_hbm, adv_hbm,
    pack_ref, logs_ref, limit_ref, own_ref, elig_ref, class_ref, scale_ref, sems,
):
    moves = (
        (elig_hbm, elig_ref),
        (class_hbm, class_ref),
        (scale_hbm, scale_ref),
        (imp_hbm, pack_ref.at[0:EMB]),
        (adv_hbm, own_ref),
    )
    copies = [pltpu.make_async_copy(src, dst, sems.at[n]) for n, (src, dst) in enumerate(moves)]
    for copy in copies:
        copy.start()
    for copy in copies:
        copy.wait()
    exponent = 0.3 * class_ref[...].astype(F32) - 1.2
    limit = ratio * jnp.exp(exponent)
    limit_ref[...] = limit
    logs_ref[...] = jnp.log(scale_ref[...]) * LOG2E + (exponent * LOG2E + math.log2(ratio / imps))
    rows, cols = class_ref.shape[0], elig_ref.shape[0]
    flags = elig_ref[...].astype(F32)
    allowance = limit / imps
    totals = []
    for c in range(cols):
        total = jnp.zeros((1, BLOCK), F32)
        for b in range(rows):
            total = total + flags[c : c + 1, b : b + 1] * allowance[b : b + 1]
        totals.append(jnp.broadcast_to(jnp.sum(total, axis=1, keepdims=True), (1, BLOCK)))
    pack_ref[EMB : EMB + 8, :] = jnp.zeros((8, pack_ref.shape[1]), F32)
    for c in range(cols):
        pack_ref[EMB + c // 2 : EMB + c // 2 + 1, c % 2 * BLOCK : (c % 2 + 1) * BLOCK] = totals[c]
    pack_ref[EMB + 4 : EMB + 4 + cols, 0:rows] = flags


def own_flags(pack_ref, cols, rows):
    return pack_ref[EMB + 4 : EMB + 4 + cols, 0:rows]


def extra_rows(flags, logs):
    cols, rows = flags.shape
    count = logs.shape[0] * BLOCK
    at = lax.broadcasted_iota(jnp.int32, (rows, count), 0)
    spread = (at == lax.broadcasted_iota(jnp.int32, (rows, count), 1) // BLOCK).astype(BF16)
    masks = (jnp.dot(flags.astype(BF16), spread, preferred_element_type=F32) - 1.0) * OFF
    line = jnp.concatenate([logs[r : r + 1] for r in range(logs.shape[0])], axis=1)
    ones = jnp.ones((1, count), F32)
    parts = [masks, *pieces(line), ones, ones, ones, jnp.zeros((10 - cols, count), F32)]
    return jnp.concatenate(parts, axis=0).astype(BF16)


def impressions_kernel(cols, rows, own_ref, down_ref, side_ref, cross_ref, logs_ref, lhs_ref, lhs_t_ref, extra_ref, price_ref):
    _, w = home()
    half = lax.axis_index("adv")
    width = own_ref.shape[1]
    count = 2 * cols * BLOCK
    places = ((own_ref, w, half), (down_ref, w, 1 - half), (side_ref, 1 - w, half), (cross_ref, 1 - w, 1 - half))
    for ref, side, part in places:
        high, low = halves(ref[0:EMB, :] * (SCORE_GAIN * LOG2E))
        at = pl.ds(pl.multiple_of(side * (2 * width) + part * width, width), width)
        lhs_ref[0:EMB, at] = high
        lhs_ref[EMB : 2 * EMB, at] = low
        lhs_ref[2 * EMB : 3 * EMB, at] = high
    rows_of = [a[EMB : EMB + 2, :] + b[EMB : EMB + 2, :] for a, b in ((own_ref, down_ref), (side_ref, cross_ref))]
    price = in_order(w, *rows_of)
    price = jnp.concatenate([price[r : r + 1] for r in range(4)], axis=1)
    column = lax.broadcasted_iota(jnp.int32, (2 * cols, count), 1) // BLOCK
    own = (column == lax.broadcasted_iota(jnp.int32, (2 * cols, count), 0)).astype(F32)
    ones = jnp.ones((1, count), F32)
    parts = [own, ones, ones, ones, *pieces(-jnp.log(price) * LOG2E), jnp.zeros((10 - 2 * cols, count), F32)]
    lhs_ref[3 * EMB :, :] = jnp.concatenate(parts, axis=0).astype(BF16)
    for c in range(2 * cols):
        price_ref[c : c + 1, :] = price[:, c * BLOCK : (c + 1) * BLOCK]
    lhs_t_ref[...] = lhs_ref[...].T
    flags = in_order(w, own_flags(own_ref, cols, rows), own_flags(side_ref, cols, rows))
    extra_ref[...] = extra_rows(flags, logs_ref[...])


def first_kernel(keys, adv_ref, extra_ref, lhs_t_ref, *refs):
    *earlier, gain_ref, sums_ref, rhs_ref = refs
    m, _ = home()
    count = gain_ref.shape[0]
    if earlier:
        sums_ref[...] = earlier[0][...]
    else:
        sums_ref[...] = jnp.zeros(sums_ref.shape, F32)
    for n in range(0, len(keys), 2):
        two = slice(n * BLOCK, (n + 2) * BLOCK)
        for p in range(2):
            lanes = slice((n + p) * BLOCK, (n + p + 1) * BLOCK)
            high, low = halves(adv_ref[n + p])
            rhs_ref[0:EMB, lanes] = high
            rhs_ref[EMB : 2 * EMB, lanes] = high
            rhs_ref[2 * EMB : 3 * EMB, lanes] = low
            at = pl.multiple_of((m ^ keys[n + p]) * BLOCK, BLOCK)
            rhs_ref[3 * EMB :, lanes] = extra_ref[:, pl.ds(at, BLOCK)]
        sums = jnp.zeros((1, 2 * BLOCK), F32)
        for h in range(2):
            part = slice(h * count // 2, (h + 1) * count // 2)
            gain = jnp.exp2(jnp.dot(lhs_t_ref[part, :], rhs_ref[:, two], preferred_element_type=F32))
            sums = sums + jnp.sum(gain, axis=0, keepdims=True)
            gain_ref[part, two] = gain
        for p in range(2):
            sums_ref[pl.ds(m ^ keys[n + p], 1), :] = sums[:, p * BLOCK : (p + 1) * BLOCK]


def rows_kernel(lhs_ref, *refs):
    *rhs_refs, gain_ref = refs
    _, w = home()
    width = gain_ref.shape[1]
    lhs = lhs_ref[:, pl.ds(pl.multiple_of(w * width, width), width)]
    at = 0
    for ref in rhs_refs:
        for lane in range(0, ref.shape[1], BLOCK):
            rhs = ref[:, lane : lane + BLOCK].T
            gain_ref[at : at + BLOCK, :] = jnp.exp2(jnp.dot(rhs, lhs, preferred_element_type=F32))
            at += BLOCK


def tiles(refs, c):
    rows = slice(c * BLOCK, (c + 1) * BLOCK)
    return [(ref, (rows, slice(lane, lane + BLOCK))) for ref in refs for lane in range(0, ref.shape[1], BLOCK)]


def prices_kernel(keys, parts, limit_ref, *refs):
    gains, sum_refs, (part_ref, pacing_ref), bids = refs[:parts], refs[parts : -2 - parts], refs[-2 - parts : -parts], refs[-parts:]
    m, _ = home()
    limit = limit_ref[...]
    pacing_ref[...] = limit / jnp.maximum(tree([ref[...] for ref in sum_refs]), limit)
    factors = [pacing_ref[pl.ds(m ^ k, 1), :] for k in keys]
    for c in range(part_ref.shape[0]):
        total = jnp.zeros((BLOCK, BLOCK), F32)
        for (gain_ref, at), (bid_ref, _), factor in zip(tiles(gains, c), tiles(bids, c), factors):
            bid = gain_ref[at] * factor
            bid_ref[at] = bid
            total = total + bid
        part_ref[c : c + 1, :] = jnp.sum(total.T, axis=0, keepdims=True)


def second_kernel(keys, parts, imps, limit_ref, pacing_ref, price_ref, *refs):
    bids, part_refs, (sums_ref, prices_ref, factor_ref, change_ref) = refs[:parts], refs[parts:-4], refs[-4:]
    m, w = home()
    prices = tree([ref[...] for ref in part_refs])
    changes = price_ref[...] / prices
    half = prices.shape[0] // 2
    prices_ref[...] = jnp.where(w == 0, prices[0:half], prices[half:])
    change = jnp.where(w == 0, changes[0:half], changes[half:])
    for c in range(half):
        change_ref[:, c * BLOCK : (c + 1) * BLOCK] = change[c : c + 1]
    factor_ref[...] = pacing_ref[...] * (imps / limit_ref[...])
    totals = [jnp.zeros((8, BLOCK), F32) for _ in keys]
    for c in range(2 * half):
        column = jnp.broadcast_to(changes[c : c + 1], (BLOCK, BLOCK)).T
        for n, (ref, at) in enumerate(tiles(bids, c)):
            bid = ref[at]
            totals[n] = totals[n] + jnp.sum((bid * (bid * column)).reshape(BLOCK // 8, 8, BLOCK), axis=0)
    for k, total in zip(keys, totals):
        sums_ref[pl.ds(m ^ k, 1), :] = jnp.sum(total, axis=0, keepdims=True)
    sums_ref[...] = sums_ref[...] * (imps / (limit_ref[...] * pacing_ref[...]))


def final_kernel(keys, advs, gain_ref, limit_ref, factor_ref, change_ref, *refs):
    *sum_refs, out_ref, pacing_out, pacing_ref, scale_ref, block_ref, sems = refs
    m, _ = home()
    limit = limit_ref[...]
    pacing = limit / jnp.maximum(tree([ref[...] for ref in sum_refs]), limit)
    scale_ref[...] = pacing * factor_ref[...] * advs
    pacing_ref[...] = pacing
    copies = [pltpu.make_async_copy(pacing_ref, pacing_out, sems.at[len(keys)])]
    copies[0].start()
    change = change_ref[...]
    shape = (BLOCK, BLOCK)
    diagonal = lax.broadcasted_iota(jnp.int32, shape, 0) == lax.broadcasted_iota(jnp.int32, shape, 1)
    for n, k in enumerate(keys):
        rows = slice(n * BLOCK, (n + 1) * BLOCK)
        scale = jnp.sum(jnp.where(diagonal, scale_ref[pl.ds(m ^ k, 1), :], 0.0), axis=1, keepdims=True)
        gain = gain_ref[rows, :]
        block_ref[rows, :] = (gain * scale) * (gain * change)
        to = pl.ds(pl.multiple_of((m ^ k) * BLOCK, BLOCK), BLOCK)
        copy = pltpu.make_async_copy(block_ref.at[rows], out_ref.at[to], sems.at[n])
        copy.start()
        copies.append(copy)
    for copy in copies:
        copy.wait()


def swap(x, axis, k):
    return lax.ppermute(x, axis, [(i, i ^ k) for i in range(lax.axis_size(axis))])


def with_partners(x, keys):
    return [x] + [swap(x, "imp", k) for k in keys]


def over_impressions(sums, stages):
    first, last = stages
    return with_partners(tree(with_partners(sums, first)), last)


def staged(adv_embed, imp_embed, value_scale, spend_class, eligible):
    adv_count = spend_class.shape[0]
    rows, cols = eligible.shape
    imp_count = cols * BLOCK
    imps, advs = imp_count * lax.axis_size("imp"), adv_count * lax.axis_size("adv")
    ratio = imps / advs

    def shape(*dims, dtype=F32):
        return jax.ShapeDtypeStruct(dims, dtype)

    def call(kernel, out, operands, cost=0, **kw):
        return pl.pallas_call(
            kernel,
            out_shape=out,
            in_specs=[VMEM] * len(operands),
            out_specs=tuple(VMEM for _ in out),
            compiler_params=PARAMS,
            cost_estimate=pl.CostEstimate(flops=cost, bytes_accessed=cost // 256, transcendentals=0),
            **kw,
        )(*operands)

    adv_t = adv_embed.T
    ins = (eligible.T, spend_class.reshape(rows, BLOCK), value_scale.reshape(rows, BLOCK), imp_embed.T, adv_t)
    ins = [pltpu.with_memory_space_constraint(x, pltpu.HBM) for x in ins]
    pack, logs, limit, own = pl.pallas_call(
        lambda *refs: prepare_kernel(ratio, imps, *refs),
        out_shape=(shape(EMB + 8, imp_embed.shape[0]), shape(rows, BLOCK), shape(rows, BLOCK), shape(*adv_t.shape)),
        in_specs=[HBM] * len(ins),
        out_specs=(VMEM,) * 4,
        scratch_shapes=[
            pltpu.VMEM((cols, rows), jnp.int32),
            pltpu.VMEM((rows, BLOCK), jnp.int32),
            pltpu.VMEM((rows, BLOCK), F32),
            pltpu.SemaphoreType.DMA((len(ins),)),
        ],
        compiler_params=PARAMS,
    )(*ins)
    line = jnp.stack([own, *with_partners(adv_t, (8, 12, 4))[1:]])
    down, side, cross = [swap(pack, ("adv", "imp"), k) for k in (16, 4, 20)]
    plane = swap(line, "imp", 2)
    plane, _ = lax.optimization_barrier((plane, (down, side, cross)))
    ready, _ = lax.optimization_barrier((line, (down, side, cross)))
    line_pair = swap(ready, "imp", 1)
    at_line = (0, 8, 12, 4)
    at_line_pair = tuple(k + 1 for k in at_line)
    at_plane = tuple(k + 2 for k in at_line)
    at_plane_pair = tuple(k + 3 for k in at_line)
    keys = at_line + at_line_pair + at_plane + at_plane_pair

    count = 2 * imp_count
    lhs, lhs_t, extra, first_price = call(
        lambda *refs: impressions_kernel(cols, rows, *refs),
        (
            shape(DEPTH, count, dtype=BF16),
            shape(count, DEPTH, dtype=BF16),
            shape(16, adv_count, dtype=BF16),
            shape(2 * cols, BLOCK),
        ),
        (pack, down, side, cross, logs),
        cost=10**8,
    )
    gains, rhs, sums = [], [], ()

    def work(at, blocks):
        nonlocal sums
        width = len(at) * BLOCK
        gain, total, side = call(
            lambda *refs: first_kernel(at, *refs),
            (pltpu.VMEM((count, width), F32), shape(rows, BLOCK), pltpu.VMEM((DEPTH, width), BF16)),
            (blocks, extra, lhs_t, *sums),
            cost=10**8 * len(at),
        )
        gains.append(gain)
        rhs.append(side)
        sums = (total,)

    work(at_line, line)
    plane, sums = lax.optimization_barrier((plane, sums))
    work(at_line_pair, line_pair)
    work(at_plane, plane)
    work(at_plane_pair, swap(plane, "imp", 1))

    terms = over_impressions(sums[0], ((8,),(1,2,3)))
    (gain_rows,) = call(rows_kernel, (pltpu.VMEM((adv_count, imp_count), F32),), (lhs, *rhs), cost=10**9)

    part, pacing, *bids = call(
        lambda *refs: prices_kernel(keys, len(gains), *refs),
        (shape(2 * cols, BLOCK), shape(rows, BLOCK), *(pltpu.VMEM(g.shape, F32) for g in gains)),
        (limit, *gains, *terms),
    )
    sums, prices, factor, change = call(
        lambda *refs: second_kernel(keys, len(gains), imps, *refs),
        (shape(rows, BLOCK), pltpu.VMEM((cols, BLOCK), F32), shape(rows, BLOCK), shape(1, imp_count)),
        (limit, pacing, first_price, *bids, part, swap(part, "adv", 1)),
    )

    terms = over_impressions(sums, ((8,),(1,2,3)))
    density, pacing = pl.pallas_call(
        lambda *refs: final_kernel(keys, advs, *refs),
        out_shape=(shape(adv_count, imp_count), shape(rows, BLOCK)),
        in_specs=[VMEM] * (4 + len(terms)),
        out_specs=(HBM, HBM),
        scratch_shapes=[
            pltpu.VMEM((rows, BLOCK), F32),
            pltpu.VMEM((rows, BLOCK), F32),
            pltpu.VMEM((adv_count, imp_count), F32),
            pltpu.SemaphoreType.DMA((rows + 1,)),
        ],
        compiler_params=PARAMS,
    )(gain_rows, limit, factor, change, *terms)
    return density, prices.reshape(imp_count), pacing.reshape(adv_count)


def plain(adv_embed, imp_embed, value_scale, spend_class, eligible):
    imp_block = lax.all_gather(imp_embed, "adv", axis=0, tiled=True)
    rows = lax.all_gather(adv_embed, "imp", axis=0, tiled=True)
    scores = SCORE_GAIN * jnp.einsum(
        "ae,ie->ai", rows, imp_block, precision=lax.Precision.HIGHEST, preferred_element_type=F32
    )
    total_advs = scores.shape[0] * lax.axis_size("adv")
    total_imps = scores.shape[1] * lax.axis_size("imp")
    mask = jnp.repeat(jnp.repeat(eligible.astype(F32), BLOCK, axis=0), BLOCK, axis=1)
    values = value_scale[:, None] * jnp.exp(scores) * mask
    allowance = total_imps / total_advs * jnp.exp(0.3 * spend_class.astype(F32) - 1.2)
    bid_tile = mask * allowance[:, None] / total_imps
    for _ in range(ITERS):
        prices = lax.psum(jnp.sum(bid_tile, axis=0), "adv")
        gain = values * bid_tile / prices[None, :]
        spending = lax.psum(jnp.sum(gain, axis=1), "imp")
        pacing = allowance / jnp.maximum(spending, allowance)
        bid_tile = pacing[:, None] * gain
    return bid_tile * total_advs, prices, pacing


def per_device(adv_embed, imp_embed, value_scale, spend_class, eligible):
    sizes = (lax.axis_size("adv"), lax.axis_size("imp"), adv_embed.shape, imp_embed.shape, eligible.shape)
    fits = sizes == (2, 16, (BLOCK, EMB), (2 * BLOCK, EMB), (16, 4))
    return (staged if fits else plain)(adv_embed, imp_embed, value_scale, spend_class, eligible)


def solution(mesh):
    in_specs = (
        P(("adv", "imp"), None),
        P(("imp", "adv"), None),
        P("adv"),
        P("adv"),
        P("adv", "imp"),
    )
    out_specs = (P("adv", "imp"), P("imp"), P("adv"))
    return jax.shard_map(
        per_device, mesh=mesh, in_specs=in_specs, out_specs=out_specs, check_vma=False
    )
```

```python
import math

import jax
import jax.numpy as jnp
from jax import lax
from jax.experimental import pallas as pl
from jax.experimental.pallas import tpu as pltpu
from jax.sharding import PartitionSpec as P

BLOCK = 128
ITERS = 2
SCORE_GAIN = 0.0875
LOG2E = 1.4426950408889634
OFF = 1e30
SMALL = 2.0**-10
EMB = 64
DEPTH = 3 * EMB + 16
F32, BF16 = jnp.float32, jnp.bfloat16

VMEM = pl.BlockSpec(memory_space=pltpu.VMEM)
HBM = pl.BlockSpec(memory_space=pltpu.HBM)
PARAMS = pltpu.CompilerParams(vmem_limit_bytes=16 * 1024 * 1024)


def home():
    m = lax.axis_index("imp")
    return m, (m >> 2) & 1


def pieces(x):
    first = x.astype(BF16).astype(F32)
    rest = x - first
    second = rest.astype(BF16).astype(F32)
    third = (rest - second).astype(BF16).astype(F32)
    return first, second, third


def halves(block):
    high = block.astype(BF16)
    return high, (block - high.astype(F32)).astype(BF16)


def tree(terms):
    while len(terms) > 1:
        terms = [a + b for a, b in zip(terms[::2], terms[1::2])]
    return terms[0]


def in_order(w, own, other):
    return jnp.concatenate([jnp.where(w == 0, own, other), jnp.where(w == 0, other, own)], axis=0)


def prepare_kernel(
    ratio, imps, elig_hbm, class_hbm, scale_hbm, imp_hbm, adv_hbm,
    pack_ref, logs_ref, limit_ref, own_ref, elig_ref, class_ref, scale_ref, sems,
):
    moves = (
        (elig_hbm, elig_ref),
        (class_hbm, class_ref),
        (scale_hbm, scale_ref),
        (imp_hbm, pack_ref.at[0:EMB]),
        (adv_hbm, own_ref),
    )
    copies = [pltpu.make_async_copy(src, dst, sems.at[n]) for n, (src, dst) in enumerate(moves)]
    for copy in copies:
        copy.start()
    for copy in copies:
        copy.wait()
    exponent = 0.3 * class_ref[...].astype(F32) - 1.2
    limit = ratio * jnp.exp(exponent)
    limit_ref[...] = limit
    logs_ref[...] = jnp.log(scale_ref[...]) * LOG2E + (exponent * LOG2E + math.log2(ratio / imps))
    rows, cols = class_ref.shape[0], elig_ref.shape[0]
    flags = elig_ref[...].astype(F32)
    allowance = limit / imps
    sums = jnp.concatenate([*pieces(allowance)], axis=1).astype(BF16)
    sums = jnp.dot(flags.astype(BF16), sums, preferred_element_type=F32)
    totals = jnp.broadcast_to(jnp.sum(sums, axis=1, keepdims=True), (cols, BLOCK))
    pack_ref[EMB : EMB + 8, :] = jnp.zeros((8, pack_ref.shape[1]), F32)
    for c in range(cols):
        pack_ref[EMB + c // 2 : EMB + c // 2 + 1, c % 2 * BLOCK : (c % 2 + 1) * BLOCK] = totals[c : c + 1]
    pack_ref[EMB + 4 : EMB + 4 + cols, 0:rows] = flags


def own_flags(pack_ref, cols, rows):
    return pack_ref[EMB + 4 : EMB + 4 + cols, 0:rows]


def extra_rows(flags, logs):
    cols, rows = flags.shape
    count = logs.shape[0] * BLOCK
    at = lax.broadcasted_iota(jnp.int32, (rows, count), 0)
    spread = (at == lax.broadcasted_iota(jnp.int32, (rows, count), 1) // BLOCK).astype(BF16)
    masks = (jnp.dot(flags.astype(BF16), spread, preferred_element_type=F32) - 1.0) * OFF
    line = jnp.concatenate([logs[r : r + 1] for r in range(logs.shape[0])], axis=1)
    ones = jnp.ones((1, count), F32)
    parts = [masks, *pieces(line), ones, ones, ones, jnp.zeros((10 - cols, count), F32)]
    return jnp.concatenate(parts, axis=0).astype(BF16)


def impressions_kernel(cols, rows, own_ref, down_ref, side_ref, cross_ref, logs_ref, lhs_ref, lhs_t_ref, extra_ref, price_ref):
    _, w = home()
    half = lax.axis_index("adv")
    width = own_ref.shape[1]
    count = 2 * cols * BLOCK
    places = ((own_ref, w, half), (down_ref, w, 1 - half), (side_ref, 1 - w, half), (cross_ref, 1 - w, 1 - half))
    for ref, side, part in places:
        high, low = halves(ref[0:EMB, :] * (SCORE_GAIN * LOG2E))
        at = pl.ds(pl.multiple_of(side * (2 * width) + part * width, width), width)
        lhs_ref[0:EMB, at] = high
        lhs_ref[EMB : 2 * EMB, at] = low
        lhs_ref[2 * EMB : 3 * EMB, at] = high
    rows_of = [a[EMB : EMB + 2, :] + b[EMB : EMB + 2, :] for a, b in ((own_ref, down_ref), (side_ref, cross_ref))]
    price = in_order(w, *rows_of)
    price = jnp.concatenate([price[r : r + 1] for r in range(4)], axis=1)
    column = lax.broadcasted_iota(jnp.int32, (2 * cols, count), 1) // BLOCK
    own = (column == lax.broadcasted_iota(jnp.int32, (2 * cols, count), 0)).astype(F32)
    ones = jnp.ones((1, count), F32)
    parts = [own, ones, ones, ones, *pieces(-jnp.log(price) * LOG2E), jnp.zeros((10 - 2 * cols, count), F32)]
    lhs_ref[3 * EMB :, :] = jnp.concatenate(parts, axis=0).astype(BF16)
    for c in range(2 * cols):
        price_ref[c : c + 1, :] = price[:, c * BLOCK : (c + 1) * BLOCK]
    lhs_t_ref[...] = lhs_ref[...].T
    flags = in_order(w, own_flags(own_ref, cols, rows), own_flags(side_ref, cols, rows))
    extra_ref[...] = extra_rows(flags, logs_ref[...])


def first_kernel(keys, adv_ref, extra_ref, lhs_t_ref, *refs):
    *earlier, gain_ref, sums_ref, rhs_ref = refs
    m, _ = home()
    count = gain_ref.shape[0]
    if earlier:
        sums_ref[...] = earlier[0][...]
    else:
        sums_ref[...] = jnp.zeros(sums_ref.shape, F32)
    for n in range(0, len(keys), 2):
        two = slice(n * BLOCK, (n + 2) * BLOCK)
        for p in range(2):
            lanes = slice((n + p) * BLOCK, (n + p + 1) * BLOCK)
            high, low = halves(adv_ref[n + p])
            rhs_ref[0:EMB, lanes] = high
            rhs_ref[EMB : 2 * EMB, lanes] = high
            rhs_ref[2 * EMB : 3 * EMB, lanes] = low
            at = pl.multiple_of((m ^ keys[n + p]) * BLOCK, BLOCK)
            rhs_ref[3 * EMB :, lanes] = extra_ref[:, pl.ds(at, BLOCK)]
        sums = jnp.zeros((1, 2 * BLOCK), F32)
        for h in range(2):
            part = slice(h * count // 2, (h + 1) * count // 2)
            gain = jnp.exp2(jnp.dot(lhs_t_ref[part, :], rhs_ref[:, two], preferred_element_type=F32))
            sums = sums + jnp.sum(gain, axis=0, keepdims=True)
            gain_ref[part, two] = gain
        for p in range(2):
            sums_ref[pl.ds(m ^ keys[n + p], 1), :] = sums[:, p * BLOCK : (p + 1) * BLOCK]


def rows_kernel(lhs_ref, *refs):
    *rhs_refs, gain_ref = refs
    _, w = home()
    width = gain_ref.shape[1]
    lhs = lhs_ref[:, pl.ds(pl.multiple_of(w * width, width), width)]
    at = 0
    for ref in rhs_refs:
        for lane in range(0, ref.shape[1], BLOCK):
            rhs = ref[:, lane : lane + BLOCK].T
            gain_ref[at : at + BLOCK, :] = jnp.exp2(jnp.dot(rhs, lhs, preferred_element_type=F32))
            at += BLOCK


def tiles(refs, c):
    rows = slice(c * BLOCK, (c + 1) * BLOCK)
    return [(ref, (rows, slice(lane, lane + BLOCK))) for ref in refs for lane in range(0, ref.shape[1], BLOCK)]


def squares_kernel(parts, *refs):
    for ref, out_ref in zip(refs[:parts], refs[parts:]):
        out_ref[...] = (ref[...] * SMALL) * (ref[...] * SMALL)


def prices_kernel(keys, parts, limit_ref, *refs):
    gains, sum_refs, (part_ref, pacing_ref) = refs[:parts], refs[parts:-2], refs[-2:]
    m, _ = home()
    limit = limit_ref[...]
    pacing_ref[...] = limit / jnp.maximum(tree([ref[...] for ref in sum_refs]), limit)
    factors = [pacing_ref[pl.ds(m ^ k, 1), :] for k in keys]
    for c in range(part_ref.shape[0]):
        total = jnp.zeros((BLOCK, BLOCK), F32)
        for (ref, at), factor in zip(tiles(gains, c), factors):
            total = total + ref[at] * factor
        part_ref[c : c + 1, :] = jnp.sum(total.T, axis=0, keepdims=True)


def second_kernel(keys, parts, imps, limit_ref, pacing_ref, price_ref, *refs):
    squares, part_refs, (sums_ref, prices_ref, factor_ref, change_ref) = refs[:parts], refs[parts:-4], refs[-4:]
    m, w = home()
    prices = tree([ref[...] for ref in part_refs])
    changes = price_ref[...] / prices
    half = prices.shape[0] // 2
    prices_ref[...] = jnp.where(w == 0, prices[0:half], prices[half:])
    change = jnp.where(w == 0, changes[0:half], changes[half:])
    for c in range(half):
        change_ref[:, c * BLOCK : (c + 1) * BLOCK] = change[c : c + 1]
    factor_ref[...] = pacing_ref[...] * (imps / limit_ref[...])
    totals = [jnp.zeros((8, BLOCK), F32) for _ in keys]
    for c in range(2 * half):
        column = jnp.broadcast_to(changes[c : c + 1], (BLOCK, BLOCK)).T
        for n, (ref, at) in enumerate(tiles(squares, c)):
            totals[n] = totals[n] + jnp.sum((ref[at] * column).reshape(BLOCK // 8, 8, BLOCK), axis=0)
    for k, total in zip(keys, totals):
        sums_ref[pl.ds(m ^ k, 1), :] = jnp.sum(total, axis=0, keepdims=True)
    sums_ref[...] = sums_ref[...] * (factor_ref[...] / SMALL**2)


def final_kernel(keys, advs, gain_ref, limit_ref, factor_ref, change_ref, *refs):
    *sum_refs, out_ref, pacing_out, pacing_ref, scale_ref, block_ref, sems = refs
    m, _ = home()
    limit = limit_ref[...]
    pacing = limit / jnp.maximum(tree([ref[...] for ref in sum_refs]), limit)
    scale_ref[...] = pacing * factor_ref[...] * advs
    pacing_ref[...] = pacing
    copies = [pltpu.make_async_copy(pacing_ref, pacing_out, sems.at[len(keys)])]
    copies[0].start()
    change = change_ref[...]
    shape = (BLOCK, BLOCK)
    diagonal = lax.broadcasted_iota(jnp.int32, shape, 0) == lax.broadcasted_iota(jnp.int32, shape, 1)
    for n, k in enumerate(keys):
        rows = slice(n * BLOCK, (n + 1) * BLOCK)
        scale = jnp.sum(jnp.where(diagonal, scale_ref[pl.ds(m ^ k, 1), :], 0.0), axis=1, keepdims=True)
        gain = gain_ref[rows, :]
        block_ref[rows, :] = (gain * scale) * (gain * change)
        to = pl.ds(pl.multiple_of((m ^ k) * BLOCK, BLOCK), BLOCK)
        copy = pltpu.make_async_copy(block_ref.at[rows], out_ref.at[to], sems.at[n])
        copy.start()
        copies.append(copy)
    for copy in copies:
        copy.wait()


def swap(x, axis, k):
    return lax.ppermute(x, axis, [(i, i ^ k) for i in range(lax.axis_size(axis))])


def with_partners(x, keys):
    return [x] + [swap(x, "imp", k) for k in keys]


def over_impressions(sums, stages):
    first, last = stages
    return with_partners(tree(with_partners(sums, first)), last)


def staged(adv_embed, imp_embed, value_scale, spend_class, eligible):
    adv_count = spend_class.shape[0]
    rows, cols = eligible.shape
    imp_count = cols * BLOCK
    imps, advs = imp_count * lax.axis_size("imp"), adv_count * lax.axis_size("adv")
    ratio = imps / advs

    def shape(*dims, dtype=F32):
        return jax.ShapeDtypeStruct(dims, dtype)

    def call(kernel, out, operands, cost=0, **kw):
        return pl.pallas_call(
            kernel,
            out_shape=out,
            in_specs=[VMEM] * len(operands),
            out_specs=tuple(VMEM for _ in out),
            compiler_params=PARAMS,
            cost_estimate=pl.CostEstimate(flops=cost, bytes_accessed=cost // 256, transcendentals=0),
            **kw,
        )(*operands)

    adv_t = adv_embed.T
    ins = (eligible.T, spend_class.reshape(rows, BLOCK), value_scale.reshape(rows, BLOCK), imp_embed.T, adv_t)
    ins = [pltpu.with_memory_space_constraint(x, pltpu.HBM) for x in ins]
    pack, logs, limit, own = pl.pallas_call(
        lambda *refs: prepare_kernel(ratio, imps, *refs),
        out_shape=(shape(EMB + 8, imp_embed.shape[0]), shape(rows, BLOCK), shape(rows, BLOCK), shape(*adv_t.shape)),
        in_specs=[HBM] * len(ins),
        out_specs=(VMEM,) * 4,
        scratch_shapes=[
            pltpu.VMEM((cols, rows), jnp.int32),
            pltpu.VMEM((rows, BLOCK), jnp.int32),
            pltpu.VMEM((rows, BLOCK), F32),
            pltpu.SemaphoreType.DMA((len(ins),)),
        ],
        compiler_params=PARAMS,
    )(*ins)
    line = jnp.stack([own, *with_partners(adv_t, (4, 12, 8))[1:]])
    down, side, cross = [swap(pack, ("adv", "imp"), k) for k in (16, 4, 20)]
    plane = swap(line, "imp", 2)
    plane, _ = lax.optimization_barrier((plane, (down, side, cross)))
    ready, _ = lax.optimization_barrier((line, (down, side, cross)))
    line_pair = swap(ready, "imp", 1)
    at_line = (0, 4, 12, 8)
    at_line_pair = tuple(k + 1 for k in at_line)
    at_plane = tuple(k + 2 for k in at_line)
    at_plane_pair = tuple(k + 3 for k in at_line)
    keys = at_line + at_line_pair + at_plane + at_plane_pair

    count = 2 * imp_count
    lhs, lhs_t, extra, first_price = call(
        lambda *refs: impressions_kernel(cols, rows, *refs),
        (
            shape(DEPTH, count, dtype=BF16),
            shape(count, DEPTH, dtype=BF16),
            shape(16, adv_count, dtype=BF16),
            shape(2 * cols, BLOCK),
        ),
        (pack, down, side, cross, logs),
        cost=10**8,
    )
    gains, rhs, sums = [], [], ()

    def work(at, blocks):
        nonlocal sums
        width = len(at) * BLOCK
        gain, total, side = call(
            lambda *refs: first_kernel(at, *refs),
            (pltpu.VMEM((count, width), F32), shape(rows, BLOCK), pltpu.VMEM((DEPTH, width), BF16)),
            (blocks, extra, lhs_t, *sums),
            cost=10**8 * len(at),
        )
        gains.append(gain)
        rhs.append(side)
        sums = (total,)

    work(at_line, line)
    plane, sums = lax.optimization_barrier((plane, sums))
    work(at_line_pair, line_pair)
    work(at_plane, plane)
    work(at_plane_pair, swap(plane, "imp", 1))

    squares = call(
        lambda *refs: squares_kernel(len(gains), *refs),
        tuple(pltpu.VMEM(g.shape, F32) for g in gains),
        gains,
        cost=10**9,
    )
    terms = over_impressions(sums[0], ((8,),(1,2,3)))
    (gain_rows,) = call(rows_kernel, (pltpu.VMEM((adv_count, imp_count), F32),), (lhs, *rhs), cost=10**9)

    part, pacing = call(
        lambda *refs: prices_kernel(keys, len(gains), *refs),
        (shape(2 * cols, BLOCK), shape(rows, BLOCK)),
        (limit, *gains, *terms),
    )
    sums, prices, factor, change = call(
        lambda *refs: second_kernel(keys, len(gains), imps, *refs),
        (shape(rows, BLOCK), pltpu.VMEM((cols, BLOCK), F32), shape(rows, BLOCK), shape(1, imp_count)),
        (limit, pacing, first_price, *squares, part, swap(part, "adv", 1)),
    )

    terms = over_impressions(sums, ((8,),(1,2,3)))
    density, pacing = pl.pallas_call(
        lambda *refs: final_kernel(keys, advs, *refs),
        out_shape=(shape(adv_count, imp_count), shape(rows, BLOCK)),
        in_specs=[VMEM] * (4 + len(terms)),
        out_specs=(HBM, HBM),
        scratch_shapes=[
            pltpu.VMEM((rows, BLOCK), F32),
            pltpu.VMEM((rows, BLOCK), F32),
            pltpu.VMEM((adv_count, imp_count), F32),
            pltpu.SemaphoreType.DMA((rows + 1,)),
        ],
        compiler_params=PARAMS,
    )(gain_rows, limit, factor, change, *terms)
    return density, prices.reshape(imp_count), pacing.reshape(adv_count)


def plain(adv_embed, imp_embed, value_scale, spend_class, eligible):
    imp_block = lax.all_gather(imp_embed, "adv", axis=0, tiled=True)
    rows = lax.all_gather(adv_embed, "imp", axis=0, tiled=True)
    scores = SCORE_GAIN * jnp.einsum(
        "ae,ie->ai", rows, imp_block, precision=lax.Precision.HIGHEST, preferred_element_type=F32
    )
    total_advs = scores.shape[0] * lax.axis_size("adv")
    total_imps = scores.shape[1] * lax.axis_size("imp")
    mask = jnp.repeat(jnp.repeat(eligible.astype(F32), BLOCK, axis=0), BLOCK, axis=1)
    values = value_scale[:, None] * jnp.exp(scores) * mask
    allowance = total_imps / total_advs * jnp.exp(0.3 * spend_class.astype(F32) - 1.2)
    bid_tile = mask * allowance[:, None] / total_imps
    for _ in range(ITERS):
        prices = lax.psum(jnp.sum(bid_tile, axis=0), "adv")
        gain = values * bid_tile / prices[None, :]
        spending = lax.psum(jnp.sum(gain, axis=1), "imp")
        pacing = allowance / jnp.maximum(spending, allowance)
        bid_tile = pacing[:, None] * gain
    return bid_tile * total_advs, prices, pacing


def per_device(adv_embed, imp_embed, value_scale, spend_class, eligible):
    sizes = (lax.axis_size("adv"), lax.axis_size("imp"), adv_embed.shape, imp_embed.shape, eligible.shape)
    fits = sizes == (2, 16, (BLOCK, EMB), (2 * BLOCK, EMB), (16, 4))
    return (staged if fits else plain)(adv_embed, imp_embed, value_scale, spend_class, eligible)


def solution(mesh):
    in_specs = (
        P(("adv", "imp"), None),
        P(("imp", "adv"), None),
        P("adv"),
        P("adv"),
        P("adv", "imp"),
    )
    out_specs = (P("adv", "imp"), P("imp"), P("adv"))
    return jax.shard_map(
        per_device, mesh=mesh, in_specs=in_specs, out_specs=out_specs, check_vma=False
    )
```

```python
import math

import jax
import jax.numpy as jnp
from jax import lax
from jax.experimental import pallas as pl
from jax.experimental.pallas import tpu as pltpu
from jax.sharding import PartitionSpec as P

BLOCK = 128
ITERS = 2
SCORE_GAIN = 0.0875
LOG2E = 1.4426950408889634
OFF = 1e30
SMALL = 2.0**-10
EMB = 64
DEPTH = 3 * EMB + 16
F32, BF16 = jnp.float32, jnp.bfloat16

VMEM = pl.BlockSpec(memory_space=pltpu.VMEM)
HBM = pl.BlockSpec(memory_space=pltpu.HBM)
PARAMS = pltpu.CompilerParams(vmem_limit_bytes=16 * 1024 * 1024)


def home():
    m = lax.axis_index("imp")
    return m, (m >> 2) & 1


def pieces(x):
    first = x.astype(BF16).astype(F32)
    rest = x - first
    second = rest.astype(BF16).astype(F32)
    third = (rest - second).astype(BF16).astype(F32)
    return first, second, third


def halves(block):
    high = block.astype(BF16)
    return high, (block - high.astype(F32)).astype(BF16)


def tree(terms):
    while len(terms) > 1:
        terms = [a + b for a, b in zip(terms[::2], terms[1::2])]
    return terms[0]


def in_order(w, own, other):
    return jnp.concatenate([jnp.where(w == 0, own, other), jnp.where(w == 0, other, own)], axis=0)


def prepare_kernel(
    ratio, imps, elig_hbm, class_hbm, scale_hbm, imp_hbm, adv_hbm,
    pack_ref, logs_ref, limit_ref, own_ref, elig_ref, class_ref, scale_ref, sems,
):
    moves = (
        (elig_hbm, elig_ref),
        (class_hbm, class_ref),
        (scale_hbm, scale_ref),
        (imp_hbm, pack_ref.at[0:EMB]),
        (adv_hbm, own_ref),
    )
    copies = [pltpu.make_async_copy(src, dst, sems.at[n]) for n, (src, dst) in enumerate(moves)]
    for copy in copies:
        copy.start()
    pack_ref[EMB : EMB + 8, :] = jnp.zeros((8, pack_ref.shape[1]), F32)
    for copy in copies:
        copy.wait()
    exponent = 0.3 * class_ref[...].astype(F32) - 1.2
    limit = ratio * jnp.exp(exponent)
    limit_ref[...] = limit
    logs_ref[...] = jnp.log(scale_ref[...]) * LOG2E + (exponent * LOG2E + math.log2(ratio / imps))
    rows, cols = class_ref.shape[0], elig_ref.shape[0]
    flags = elig_ref[...].astype(F32)
    allowance = limit / imps
    sums = sum(jnp.dot(flags.astype(BF16), p.astype(BF16), preferred_element_type=F32) for p in pieces(allowance))
    pack_ref[EMB : EMB + cols, 0:BLOCK] = sums
    pack_ref[EMB + 4 : EMB + 4 + cols, 0:rows] = flags


def own_flags(pack_ref, cols, rows):
    return pack_ref[EMB + 4 : EMB + 4 + cols, 0:rows]


def extra_rows(flags, logs):
    cols, rows = flags.shape
    count = logs.shape[0] * BLOCK
    at = lax.broadcasted_iota(jnp.int32, (rows, count), 0)
    spread = (at == lax.broadcasted_iota(jnp.int32, (rows, count), 1) // BLOCK).astype(BF16)
    masks = (jnp.dot(flags.astype(BF16), spread, preferred_element_type=F32) - 1.0) * OFF
    line = jnp.concatenate([logs[r : r + 1] for r in range(logs.shape[0])], axis=1)
    ones = jnp.ones((1, count), F32)
    parts = [masks, *pieces(line), ones, ones, ones, jnp.zeros((10 - cols, count), F32)]
    return jnp.concatenate(parts, axis=0).astype(BF16)


def impressions_kernel(cols, rows, own_ref, down_ref, side_ref, cross_ref, logs_ref, lhs_ref, lhs_t_ref, extra_ref, price_ref):
    _, w = home()
    half = lax.axis_index("adv")
    width = own_ref.shape[1]
    count = 2 * cols * BLOCK
    places = ((own_ref, w, half), (down_ref, w, 1 - half), (side_ref, 1 - w, half), (cross_ref, 1 - w, 1 - half))
    for ref, side, part in places:
        high, low = halves(ref[0:EMB, :] * (SCORE_GAIN * LOG2E))
        at = pl.ds(pl.multiple_of(side * (2 * width) + part * width, width), width)
        lhs_ref[0:EMB, at] = high
        lhs_ref[EMB : 2 * EMB, at] = low
        lhs_ref[2 * EMB : 3 * EMB, at] = high
    lanes = [a[EMB : EMB + cols, 0:BLOCK] + b[EMB : EMB + cols, 0:BLOCK] for a, b in ((own_ref, down_ref), (side_ref, cross_ref))]
    totals = jnp.sum(in_order(w, *lanes), axis=1, keepdims=True)
    price_ref[...] = jnp.broadcast_to(totals, price_ref.shape)
    price = jnp.concatenate([price_ref[c : c + 1, :] for c in range(2 * cols)], axis=1)
    column = lax.broadcasted_iota(jnp.int32, (2 * cols, count), 1) // BLOCK
    own = (column == lax.broadcasted_iota(jnp.int32, (2 * cols, count), 0)).astype(F32)
    ones = jnp.ones((1, count), F32)
    parts = [own, ones, ones, ones, *pieces(-jnp.log(price) * LOG2E), jnp.zeros((10 - 2 * cols, count), F32)]
    lhs_ref[3 * EMB :, :] = jnp.concatenate(parts, axis=0).astype(BF16)
    lhs_t_ref[...] = lhs_ref[...].T
    flags = in_order(w, own_flags(own_ref, cols, rows), own_flags(side_ref, cols, rows))
    extra_ref[...] = extra_rows(flags, logs_ref[...])


def first_kernel(keys, adv_ref, extra_ref, lhs_t_ref, *refs):
    *earlier, gain_ref, sums_ref, rhs_ref = refs
    m, _ = home()
    count = gain_ref.shape[0]
    if earlier:
        sums_ref[...] = earlier[0][...]
    else:
        sums_ref[...] = jnp.zeros(sums_ref.shape, F32)
    for n in range(0, len(keys), 2):
        two = slice(n * BLOCK, (n + 2) * BLOCK)
        for p in range(2):
            lanes = slice((n + p) * BLOCK, (n + p + 1) * BLOCK)
            high, low = halves(adv_ref[n + p])
            rhs_ref[0:EMB, lanes] = high
            rhs_ref[EMB : 2 * EMB, lanes] = high
            rhs_ref[2 * EMB : 3 * EMB, lanes] = low
            at = pl.multiple_of((m ^ keys[n + p]) * BLOCK, BLOCK)
            rhs_ref[3 * EMB :, lanes] = extra_ref[:, pl.ds(at, BLOCK)]
        sums = jnp.zeros((1, 2 * BLOCK), F32)
        for h in range(2):
            part = slice(h * count // 2, (h + 1) * count // 2)
            gain = jnp.exp2(jnp.dot(lhs_t_ref[part, :], rhs_ref[:, two], preferred_element_type=F32))
            sums = sums + jnp.sum(gain, axis=0, keepdims=True)
            gain_ref[part, two] = gain
        for p in range(2):
            sums_ref[pl.ds(m ^ keys[n + p], 1), :] = sums[:, p * BLOCK : (p + 1) * BLOCK]


def rows_kernel(lhs_ref, *refs):
    *rhs_refs, gain_ref = refs
    _, w = home()
    width = gain_ref.shape[1]
    lhs = lhs_ref[:, pl.ds(pl.multiple_of(w * width, width), width)]
    at = 0
    for ref in rhs_refs:
        for lane in range(0, ref.shape[1], BLOCK):
            rhs = ref[:, lane : lane + BLOCK].T
            gain_ref[at : at + BLOCK, :] = jnp.exp2(jnp.dot(rhs, lhs, preferred_element_type=F32))
            at += BLOCK


def tiles(refs, c):
    rows = slice(c * BLOCK, (c + 1) * BLOCK)
    return [(ref, (rows, slice(lane, lane + BLOCK))) for ref in refs for lane in range(0, ref.shape[1], BLOCK)]


def squares_kernel(parts, *refs):
    for ref, out_ref in zip(refs[:parts], refs[parts:]):
        out_ref[...] = (ref[...] * SMALL) * (ref[...] * SMALL)


def prices_kernel(keys, parts, limit_ref, *refs):
    gains, sum_refs, (part_ref, pacing_ref) = refs[:parts], refs[parts:-2], refs[-2:]
    m, _ = home()
    limit = limit_ref[...]
    pacing_ref[...] = limit / jnp.maximum(tree([ref[...] for ref in sum_refs]), limit)
    factors = [pacing_ref[pl.ds(m ^ k, 1), :] for k in keys]
    for c in range(part_ref.shape[0]):
        total = jnp.zeros((BLOCK, BLOCK), F32)
        paced = [ref[at] * factor for (ref, at), factor in zip(tiles(gains, c), factors)]
        for one, two in zip(paced[::2], paced[1::2]):
            total = total + (one + two)
        part_ref[c : c + 1, :] = jnp.sum(total.T, axis=0, keepdims=True)


def second_kernel(keys, parts, imps, limit_ref, pacing_ref, price_ref, *refs):
    squares, part_refs, (sums_ref, prices_ref, factor_ref, change_ref) = refs[:parts], refs[parts:-4], refs[-4:]
    m, w = home()
    prices = tree([ref[...] for ref in part_refs])
    changes = price_ref[...] / prices
    half = prices.shape[0] // 2
    prices_ref[...] = jnp.where(w == 0, prices[0:half], prices[half:])
    change = jnp.where(w == 0, changes[0:half], changes[half:])
    for c in range(half):
        change_ref[:, c * BLOCK : (c + 1) * BLOCK] = change[c : c + 1]
    factor_ref[...] = pacing_ref[...] * (imps / limit_ref[...])
    totals = [jnp.zeros((8, BLOCK), F32) for _ in keys]
    for c in range(2 * half):
        column = jnp.broadcast_to(changes[c : c + 1], (BLOCK, BLOCK)).T
        for n, (ref, at) in enumerate(tiles(squares, c)):
            totals[n] = totals[n] + jnp.sum((ref[at] * column).reshape(BLOCK // 8, 8, BLOCK), axis=0)
    for k, total in zip(keys, totals):
        sums_ref[pl.ds(m ^ k, 1), :] = jnp.sum(total, axis=0, keepdims=True)
    sums_ref[...] = sums_ref[...] * (factor_ref[...] / SMALL**2)


def final_kernel(keys, advs, gain_ref, limit_ref, factor_ref, change_ref, *refs):
    *sum_refs, out_ref, pacing_out, pacing_ref, scale_ref, block_ref, sems = refs
    m, _ = home()
    limit = limit_ref[...]
    pacing = limit / jnp.maximum(tree([ref[...] for ref in sum_refs]), limit)
    scale_ref[...] = pacing * factor_ref[...] * advs
    pacing_ref[...] = pacing
    copies = [pltpu.make_async_copy(pacing_ref, pacing_out, sems.at[len(keys)])]
    copies[0].start()
    change = change_ref[...]
    shape = (BLOCK, BLOCK)
    diagonal = lax.broadcasted_iota(jnp.int32, shape, 0) == lax.broadcasted_iota(jnp.int32, shape, 1)
    for n, k in enumerate(keys):
        rows = slice(n * BLOCK, (n + 1) * BLOCK)
        scale = jnp.sum(jnp.where(diagonal, scale_ref[pl.ds(m ^ k, 1), :], 0.0), axis=1, keepdims=True)
        gain = gain_ref[rows, :]
        block_ref[rows, :] = (gain * scale) * (gain * change)
        to = pl.ds(pl.multiple_of((m ^ k) * BLOCK, BLOCK), BLOCK)
        copy = pltpu.make_async_copy(block_ref.at[rows], out_ref.at[to], sems.at[n])
        copy.start()
        copies.append(copy)
    for copy in copies:
        copy.wait()


def swap(x, axis, k):
    return lax.ppermute(x, axis, [(i, i ^ k) for i in range(lax.axis_size(axis))])


def with_partners(x, keys):
    return [x] + [swap(x, "imp", k) for k in keys]


def over_impressions(sums, stages):
    first, last = stages
    return with_partners(tree(with_partners(sums, first)), last)


def staged(adv_embed, imp_embed, value_scale, spend_class, eligible):
    adv_count = spend_class.shape[0]
    rows, cols = eligible.shape
    imp_count = cols * BLOCK
    imps, advs = imp_count * lax.axis_size("imp"), adv_count * lax.axis_size("adv")
    ratio = imps / advs

    def shape(*dims, dtype=F32):
        return jax.ShapeDtypeStruct(dims, dtype)

    def call(kernel, out, operands, cost=0, **kw):
        return pl.pallas_call(
            kernel,
            out_shape=out,
            in_specs=[VMEM] * len(operands),
            out_specs=tuple(VMEM for _ in out),
            compiler_params=PARAMS,
            cost_estimate=pl.CostEstimate(flops=cost, bytes_accessed=cost // 256, transcendentals=0),
            **kw,
        )(*operands)

    adv_t = adv_embed.T
    ins = (eligible.T, spend_class.reshape(rows, BLOCK), value_scale.reshape(rows, BLOCK), imp_embed.T, adv_t)
    ins = [pltpu.with_memory_space_constraint(x, pltpu.HBM) for x in ins]
    pack, logs, limit, own = pl.pallas_call(
        lambda *refs: prepare_kernel(ratio, imps, *refs),
        out_shape=(shape(EMB + 8, imp_embed.shape[0]), shape(rows, BLOCK), shape(rows, BLOCK), shape(*adv_t.shape)),
        in_specs=[HBM] * len(ins),
        out_specs=(VMEM,) * 4,
        scratch_shapes=[
            pltpu.VMEM((cols, rows), jnp.int32),
            pltpu.VMEM((rows, BLOCK), jnp.int32),
            pltpu.VMEM((rows, BLOCK), F32),
            pltpu.SemaphoreType.DMA((len(ins),)),
        ],
        compiler_params=PARAMS,
    )(*ins)
    line = jnp.stack([own, *with_partners(adv_t, (4, 12, 8))[1:]])
    down, side, cross = [swap(pack, ("adv", "imp"), k) for k in (16, 4, 20)]
    plane = swap(line, "imp", 2)
    plane, _ = lax.optimization_barrier((plane, (down, side, cross)))
    ready, _ = lax.optimization_barrier((line, (down, side, cross)))
    line_pair = swap(ready, "imp", 1)
    at_line = (0, 4, 12, 8)
    at_line_pair = tuple(k + 1 for k in at_line)
    at_plane = tuple(k + 2 for k in at_line)
    at_plane_pair = tuple(k + 3 for k in at_line)
    keys = at_line + at_line_pair + at_plane + at_plane_pair

    count = 2 * imp_count
    lhs, lhs_t, extra, first_price = call(
        lambda *refs: impressions_kernel(cols, rows, *refs),
        (
            shape(DEPTH, count, dtype=BF16),
            shape(count, DEPTH, dtype=BF16),
            shape(16, adv_count, dtype=BF16),
            shape(2 * cols, BLOCK),
        ),
        (pack, down, side, cross, logs),
        cost=10**8,
    )
    gains, rhs, sums = [], [], ()

    def work(at, blocks):
        nonlocal sums
        width = len(at) * BLOCK
        gain, total, side = call(
            lambda *refs: first_kernel(at, *refs),
            (pltpu.VMEM((count, width), F32), shape(rows, BLOCK), pltpu.VMEM((DEPTH, width), BF16)),
            (blocks, extra, lhs_t, *sums),
            cost=10**8 * len(at),
        )
        gains.append(gain)
        rhs.append(side)
        sums = (total,)

    work(at_line, line)
    plane, sums = lax.optimization_barrier((plane, sums))
    work(at_line_pair, line_pair)
    work(at_plane, plane)
    work(at_plane_pair, swap(plane, "imp", 1))

    squares = call(
        lambda *refs: squares_kernel(len(gains), *refs),
        tuple(pltpu.VMEM(g.shape, F32) for g in gains),
        gains,
        cost=10**9,
    )
    terms = over_impressions(sums[0], ((8,),(1,2,3)))
    (gain_rows,) = call(rows_kernel, (pltpu.VMEM((adv_count, imp_count), F32),), (lhs, *rhs), cost=10**9)

    part, pacing = call(
        lambda *refs: prices_kernel(keys, len(gains), *refs),
        (shape(2 * cols, BLOCK), shape(rows, BLOCK)),
        (limit, *gains, *terms),
    )
    sums, prices, factor, change = call(
        lambda *refs: second_kernel(keys, len(gains), imps, *refs),
        (shape(rows, BLOCK), pltpu.VMEM((cols, BLOCK), F32), shape(rows, BLOCK), shape(1, imp_count)),
        (limit, pacing, first_price, *squares, part, swap(part, "adv", 1)),
    )

    terms = over_impressions(sums, ((8,),(1,2,3)))
    density, pacing = pl.pallas_call(
        lambda *refs: final_kernel(keys, advs, *refs),
        out_shape=(shape(adv_count, imp_count), shape(rows, BLOCK)),
        in_specs=[VMEM] * (4 + len(terms)),
        out_specs=(HBM, HBM),
        scratch_shapes=[
            pltpu.VMEM((rows, BLOCK), F32),
            pltpu.VMEM((rows, BLOCK), F32),
            pltpu.VMEM((adv_count, imp_count), F32),
            pltpu.SemaphoreType.DMA((rows + 1,)),
        ],
        compiler_params=PARAMS,
    )(gain_rows, limit, factor, change, *terms)
    return density, prices.reshape(imp_count), pacing.reshape(adv_count)


def plain(adv_embed, imp_embed, value_scale, spend_class, eligible):
    imp_block = lax.all_gather(imp_embed, "adv", axis=0, tiled=True)
    rows = lax.all_gather(adv_embed, "imp", axis=0, tiled=True)
    scores = SCORE_GAIN * jnp.einsum(
        "ae,ie->ai", rows, imp_block, precision=lax.Precision.HIGHEST, preferred_element_type=F32
    )
    total_advs = scores.shape[0] * lax.axis_size("adv")
    total_imps = scores.shape[1] * lax.axis_size("imp")
    mask = jnp.repeat(jnp.repeat(eligible.astype(F32), BLOCK, axis=0), BLOCK, axis=1)
    values = value_scale[:, None] * jnp.exp(scores) * mask
    allowance = total_imps / total_advs * jnp.exp(0.3 * spend_class.astype(F32) - 1.2)
    bid_tile = mask * allowance[:, None] / total_imps
    for _ in range(ITERS):
        prices = lax.psum(jnp.sum(bid_tile, axis=0), "adv")
        gain = values * bid_tile / prices[None, :]
        spending = lax.psum(jnp.sum(gain, axis=1), "imp")
        pacing = allowance / jnp.maximum(spending, allowance)
        bid_tile = pacing[:, None] * gain
    return bid_tile * total_advs, prices, pacing


def per_device(adv_embed, imp_embed, value_scale, spend_class, eligible):
    sizes = (lax.axis_size("adv"), lax.axis_size("imp"), adv_embed.shape, imp_embed.shape, eligible.shape)
    fits = sizes == (2, 16, (BLOCK, EMB), (2 * BLOCK, EMB), (16, 4))
    return (staged if fits else plain)(adv_embed, imp_embed, value_scale, spend_class, eligible)


def solution(mesh):
    in_specs = (
        P(("adv", "imp"), None),
        P(("imp", "adv"), None),
        P("adv"),
        P("adv"),
        P("adv", "imp"),
    )
    out_specs = (P("adv", "imp"), P("imp"), P("adv"))
    return jax.shard_map(
        per_device, mesh=mesh, in_specs=in_specs, out_specs=out_specs, check_vma=False
    )
```

```python
import math

import jax
import jax.numpy as jnp
from jax import lax
from jax.experimental import pallas as pl
from jax.experimental.pallas import tpu as pltpu
from jax.sharding import PartitionSpec as P

BLOCK = 128
ITERS = 2
SCORE_GAIN = 0.0875
LOG2E = 1.4426950408889634
OFF = 1e30
SMALL = 2.0**-10
EMB = 64
DEPTH = 3 * EMB + 16
F32, BF16 = jnp.float32, jnp.bfloat16

VMEM = pl.BlockSpec(memory_space=pltpu.VMEM)
HBM = pl.BlockSpec(memory_space=pltpu.HBM)
PARAMS = pltpu.CompilerParams(vmem_limit_bytes=16 * 1024 * 1024)


def home():
    m = lax.axis_index("imp")
    return m, (m >> 2) & 1


def pieces(x):
    first = x.astype(BF16).astype(F32)
    rest = x - first
    second = rest.astype(BF16).astype(F32)
    third = (rest - second).astype(BF16).astype(F32)
    return first, second, third


def halves(block):
    high = block.astype(BF16)
    return high, (block - high.astype(F32)).astype(BF16)


def tree(terms):
    while len(terms) > 1:
        terms = [a + b for a, b in zip(terms[::2], terms[1::2])]
    return terms[0]


def in_order(w, own, other):
    return jnp.concatenate([jnp.where(w == 0, own, other), jnp.where(w == 0, other, own)], axis=0)


def prepare_kernel(
    ratio, imps, elig_hbm, class_hbm, scale_hbm, imp_hbm, adv_hbm,
    pack_ref, class_ref, scale_ref, own_ref, elig_ref, sems,
):
    moves = (
        (elig_hbm, elig_ref),
        (class_hbm, class_ref),
        (scale_hbm, scale_ref),
        (imp_hbm, pack_ref.at[0:EMB]),
        (adv_hbm, own_ref),
    )
    copies = [pltpu.make_async_copy(src, dst, sems.at[n]) for n, (src, dst) in enumerate(moves)]
    for copy in copies:
        copy.start()
    pack_ref[EMB : EMB + 8, :] = jnp.zeros((8, pack_ref.shape[1]), F32)
    for copy in copies:
        copy.wait()
    limit = ratio * jnp.exp(0.3 * class_ref[...].astype(F32) - 1.2)
    rows, cols = class_ref.shape[0], elig_ref.shape[0]
    flags = elig_ref[...].astype(F32)
    allowance = limit / imps
    sums = sum(jnp.dot(flags.astype(BF16), p.astype(BF16), preferred_element_type=F32) for p in pieces(allowance))
    pack_ref[EMB : EMB + cols, 0:BLOCK] = sums
    pack_ref[EMB + 4 : EMB + 4 + cols, 0:rows] = flags


def own_flags(pack_ref, cols, rows):
    return pack_ref[EMB + 4 : EMB + 4 + cols, 0:rows]


def extra_rows(flags, logs):
    cols, rows = flags.shape
    count = logs.shape[0] * BLOCK
    at = lax.broadcasted_iota(jnp.int32, (rows, count), 0)
    spread = (at == lax.broadcasted_iota(jnp.int32, (rows, count), 1) // BLOCK).astype(BF16)
    masks = (jnp.dot(flags.astype(BF16), spread, preferred_element_type=F32) - 1.0) * OFF
    line = jnp.concatenate([logs[r : r + 1] for r in range(logs.shape[0])], axis=1)
    ones = jnp.ones((1, count), F32)
    parts = [masks, *pieces(line), ones, ones, ones, jnp.zeros((10 - cols, count), F32)]
    return jnp.concatenate(parts, axis=0).astype(BF16)


def impressions_kernel(
    cols, rows, ratio, imps, own_ref, down_ref, side_ref, cross_ref, class_ref, scale_ref,
    lhs_ref, lhs_t_ref, extra_ref, price_ref, limit_ref,
):
    _, w = home()
    half = lax.axis_index("adv")
    width = own_ref.shape[1]
    count = 2 * cols * BLOCK
    places = ((own_ref, w, half), (down_ref, w, 1 - half), (side_ref, 1 - w, half), (cross_ref, 1 - w, 1 - half))
    for ref, side, part in places:
        high, low = halves(ref[0:EMB, :] * (SCORE_GAIN * LOG2E))
        at = pl.ds(pl.multiple_of(side * (2 * width) + part * width, width), width)
        lhs_ref[0:EMB, at] = high
        lhs_ref[EMB : 2 * EMB, at] = low
        lhs_ref[2 * EMB : 3 * EMB, at] = high
    lanes = [a[EMB : EMB + cols, 0:BLOCK] + b[EMB : EMB + cols, 0:BLOCK] for a, b in ((own_ref, down_ref), (side_ref, cross_ref))]
    totals = jnp.sum(in_order(w, *lanes), axis=1, keepdims=True)
    price_ref[...] = jnp.broadcast_to(totals, price_ref.shape)
    price = jnp.concatenate([price_ref[c : c + 1, :] for c in range(2 * cols)], axis=1)
    column = lax.broadcasted_iota(jnp.int32, (2 * cols, count), 1) // BLOCK
    own = (column == lax.broadcasted_iota(jnp.int32, (2 * cols, count), 0)).astype(F32)
    ones = jnp.ones((1, count), F32)
    parts = [own, ones, ones, ones, *pieces(-jnp.log(price) * LOG2E), jnp.zeros((10 - 2 * cols, count), F32)]
    lhs_ref[3 * EMB :, :] = jnp.concatenate(parts, axis=0).astype(BF16)
    lhs_t_ref[...] = lhs_ref[...].T
    flags = in_order(w, own_flags(own_ref, cols, rows), own_flags(side_ref, cols, rows))
    exponent = 0.3 * class_ref[...].astype(F32) - 1.2
    limit_ref[...] = ratio * jnp.exp(exponent)
    logs = jnp.log(scale_ref[...]) * LOG2E + (exponent * LOG2E + math.log2(ratio / imps))
    extra_ref[...] = extra_rows(flags, logs)


def first_kernel(keys, adv_ref, extra_ref, lhs_t_ref, *refs):
    *earlier, gain_ref, sums_ref, rhs_ref = refs
    m, _ = home()
    count = gain_ref.shape[0]
    if earlier:
        sums_ref[...] = earlier[0][...]
    else:
        sums_ref[...] = jnp.zeros(sums_ref.shape, F32)
    for n in range(0, len(keys), 2):
        two = slice(n * BLOCK, (n + 2) * BLOCK)
        for p in range(2):
            lanes = slice((n + p) * BLOCK, (n + p + 1) * BLOCK)
            high, low = halves(adv_ref[n + p])
            rhs_ref[0:EMB, lanes] = high
            rhs_ref[EMB : 2 * EMB, lanes] = high
            rhs_ref[2 * EMB : 3 * EMB, lanes] = low
            at = pl.multiple_of((m ^ keys[n + p]) * BLOCK, BLOCK)
            rhs_ref[3 * EMB :, lanes] = extra_ref[:, pl.ds(at, BLOCK)]
        sums = jnp.zeros((1, 2 * BLOCK), F32)
        for h in range(2):
            part = slice(h * count // 2, (h + 1) * count // 2)
            gain = jnp.exp2(jnp.dot(lhs_t_ref[part, :], rhs_ref[:, two], preferred_element_type=F32))
            sums = sums + jnp.sum(gain, axis=0, keepdims=True)
            gain_ref[part, two] = gain
        for p in range(2):
            sums_ref[pl.ds(m ^ keys[n + p], 1), :] = sums[:, p * BLOCK : (p + 1) * BLOCK]


def as_column(row):
    shape = (BLOCK, BLOCK)
    diagonal = lax.broadcasted_iota(jnp.int32, shape, 0) == lax.broadcasted_iota(jnp.int32, shape, 1)
    return jnp.sum(jnp.where(diagonal, row, 0.0), axis=1, keepdims=True)


def rows_kernel(keys, advs, lhs_ref, factor_ref, change_ref, *refs):
    *rhs_refs, out_ref = refs
    m, w = home()
    width = out_ref.shape[1]
    lhs = lhs_ref[:, pl.ds(pl.multiple_of(w * width, width), width)]
    change = change_ref[...]
    blocks = [(ref, lane) for ref in rhs_refs for lane in range(0, ref.shape[1], BLOCK)]
    for n, (ref, lane) in enumerate(blocks):
        gain = jnp.exp2(jnp.dot(ref[:, lane : lane + BLOCK].T, lhs, preferred_element_type=F32))
        factor = as_column(factor_ref[pl.ds(m ^ keys[n], 1), :] * advs)
        out_ref[n * BLOCK : (n + 1) * BLOCK, :] = (gain * factor) * (gain * change)


def tiles(refs, c):
    rows = slice(c * BLOCK, (c + 1) * BLOCK)
    return [(ref, (rows, slice(lane, lane + BLOCK))) for ref in refs for lane in range(0, ref.shape[1], BLOCK)]


def squares_kernel(parts, *refs):
    for ref, out_ref in zip(refs[:parts], refs[parts:]):
        out_ref[...] = (ref[...] * SMALL) * (ref[...] * SMALL)


def prices_kernel(keys, parts, limit_ref, *refs):
    gains, sum_refs, (part_ref, pacing_ref) = refs[:parts], refs[parts:-2], refs[-2:]
    m, _ = home()
    limit = limit_ref[...]
    pacing_ref[...] = limit / jnp.maximum(tree([ref[...] for ref in sum_refs]), limit)
    factors = [pacing_ref[pl.ds(m ^ k, 1), :] for k in keys]
    for c in range(part_ref.shape[0]):
        total = jnp.zeros((BLOCK, BLOCK), F32)
        paced = [ref[at] * factor for (ref, at), factor in zip(tiles(gains, c), factors)]
        for one, two in zip(paced[::2], paced[1::2]):
            total = total + (one + two)
        part_ref[c : c + 1, :] = jnp.sum(total.T, axis=0, keepdims=True)


def second_kernel(keys, parts, imps, limit_ref, pacing_ref, price_ref, *refs):
    squares, part_refs, (sums_ref, prices_ref, factor_ref, change_ref) = refs[:parts], refs[parts:-4], refs[-4:]
    m, w = home()
    prices = tree([ref[...] for ref in part_refs])
    changes = price_ref[...] / prices
    half = prices.shape[0] // 2
    prices_ref[...] = jnp.where(w == 0, prices[0:half], prices[half:])
    change = jnp.where(w == 0, changes[0:half], changes[half:])
    for c in range(half):
        change_ref[:, c * BLOCK : (c + 1) * BLOCK] = change[c : c + 1]
    factor_ref[...] = pacing_ref[...] * (imps / limit_ref[...])
    totals = [jnp.zeros((8, BLOCK), F32) for _ in keys]
    for c in range(2 * half):
        column = jnp.broadcast_to(changes[c : c + 1], (BLOCK, BLOCK)).T
        for n, (ref, at) in enumerate(tiles(squares, c)):
            totals[n] = totals[n] + jnp.sum((ref[at] * column).reshape(BLOCK // 8, 8, BLOCK), axis=0)
    for k, total in zip(keys, totals):
        sums_ref[pl.ds(m ^ k, 1), :] = jnp.sum(total, axis=0, keepdims=True)
    sums_ref[...] = sums_ref[...] * (factor_ref[...] / SMALL**2)


def final_kernel(keys, gain_ref, limit_ref, *refs):
    *sum_refs, out_ref, pacing_out, pacing_ref, block_ref, sems = refs
    m, _ = home()
    limit = limit_ref[...]
    pacing_ref[...] = limit / jnp.maximum(tree([ref[...] for ref in sum_refs]), limit)
    copies = []
    for n, k in enumerate(keys):
        rows = slice(n * BLOCK, (n + 1) * BLOCK)
        block_ref[rows, :] = gain_ref[rows, :] * as_column(pacing_ref[pl.ds(m ^ k, 1), :])
        to = pl.ds(pl.multiple_of((m ^ k) * BLOCK, BLOCK), BLOCK)
        copies.append(pltpu.make_async_copy(block_ref.at[rows], out_ref.at[to], sems.at[n]))
        copies[-1].start()
    copies.append(pltpu.make_async_copy(pacing_ref, pacing_out, sems.at[len(keys)]))
    copies[-1].start()
    for copy in copies:
        copy.wait()


def swap(x, axis, k):
    return lax.ppermute(x, axis, [(i, i ^ k) for i in range(lax.axis_size(axis))])


def with_partners(x, keys):
    return [x] + [swap(x, "imp", k) for k in keys]


def over_impressions(sums, stages):
    first, last = stages
    return with_partners(tree(with_partners(sums, first)), last)


def staged(adv_embed, imp_embed, value_scale, spend_class, eligible):
    adv_count = spend_class.shape[0]
    rows, cols = eligible.shape
    imp_count = cols * BLOCK
    imps, advs = imp_count * lax.axis_size("imp"), adv_count * lax.axis_size("adv")
    ratio = imps / advs

    def shape(*dims, dtype=F32):
        return jax.ShapeDtypeStruct(dims, dtype)

    def call(kernel, out, operands, cost=0, **kw):
        return pl.pallas_call(
            kernel,
            out_shape=out,
            in_specs=[VMEM] * len(operands),
            out_specs=tuple(VMEM for _ in out),
            compiler_params=PARAMS,
            cost_estimate=pl.CostEstimate(flops=cost, bytes_accessed=cost // 256, transcendentals=0),
            **kw,
        )(*operands)

    adv_t = adv_embed.T
    ins = (eligible.T, spend_class.reshape(rows, BLOCK), value_scale.reshape(rows, BLOCK), imp_embed.T, adv_t)
    ins = [pltpu.with_memory_space_constraint(x, pltpu.HBM) for x in ins]
    pack, classes, scales, own = pl.pallas_call(
        lambda *refs: prepare_kernel(ratio, imps, *refs),
        out_shape=(shape(EMB + 8, imp_embed.shape[0]), shape(rows, BLOCK, dtype=jnp.int32), shape(rows, BLOCK), shape(*adv_t.shape)),
        in_specs=[HBM] * len(ins),
        out_specs=(VMEM,) * 4,
        scratch_shapes=[
            pltpu.VMEM((cols, rows), jnp.int32),
            pltpu.SemaphoreType.DMA((len(ins),)),
        ],
        compiler_params=PARAMS,
    )(*ins)
    line = jnp.stack([own, *with_partners(adv_t, (4, 12, 8))[1:]])
    down, side, cross = [swap(pack, ("adv", "imp"), k) for k in (16, 4, 20)]
    plane = swap(line, "imp", 2)
    plane, _ = lax.optimization_barrier((plane, (down, side, cross)))
    ready, _ = lax.optimization_barrier((line, (down, side, cross)))
    line_pair = swap(ready, "imp", 1)
    at_line = (0, 4, 12, 8)
    at_line_pair = tuple(k + 1 for k in at_line)
    at_plane = tuple(k + 2 for k in at_line)
    at_plane_pair = tuple(k + 3 for k in at_line)
    keys = at_line + at_line_pair + at_plane + at_plane_pair

    count = 2 * imp_count
    lhs, lhs_t, extra, first_price, limit = call(
        lambda *refs: impressions_kernel(cols, rows, ratio, imps, *refs),
        (
            shape(DEPTH, count, dtype=BF16),
            shape(count, DEPTH, dtype=BF16),
            shape(16, adv_count, dtype=BF16),
            shape(2 * cols, BLOCK),
            shape(rows, BLOCK),
        ),
        (pack, down, side, cross, classes, scales),
        cost=10**8,
    )
    gains, rhs, sums = [], [], ()

    def work(at, blocks):
        nonlocal sums
        width = len(at) * BLOCK
        gain, total, side = call(
            lambda *refs: first_kernel(at, *refs),
            (pltpu.VMEM((count, width), F32), shape(rows, BLOCK), pltpu.VMEM((DEPTH, width), BF16)),
            (blocks, extra, lhs_t, *sums),
            cost=10**8 * len(at),
        )
        gains.append(gain)
        rhs.append(side)
        sums = (total,)

    work(at_line, line)
    plane, sums = lax.optimization_barrier((plane, sums))
    work(at_line_pair, line_pair)
    work(at_plane, plane)
    work(at_plane_pair, swap(plane, "imp", 1))

    squares = call(
        lambda *refs: squares_kernel(len(gains), *refs),
        tuple(pltpu.VMEM(g.shape, F32) for g in gains),
        gains,
        cost=10**9,
    )
    terms = over_impressions(sums[0], ((8,),(1,2,3)))

    part, pacing = call(
        lambda *refs: prices_kernel(keys, len(gains), *refs),
        (shape(2 * cols, BLOCK), shape(rows, BLOCK)),
        (limit, *gains, *terms),
    )
    sums, prices, factor, change = call(
        lambda *refs: second_kernel(keys, len(gains), imps, *refs),
        (shape(rows, BLOCK), pltpu.VMEM((cols, BLOCK), F32), shape(rows, BLOCK), shape(1, imp_count)),
        (limit, pacing, first_price, *squares, part, swap(part, "adv", 1)),
    )

    terms = over_impressions(sums, ((8,),(1,2,3)))
    (gain_rows,) = call(
        lambda *refs: rows_kernel(keys, advs, *refs),
        (pltpu.VMEM((adv_count, imp_count), F32),),
        (lhs, factor, change, *rhs),
        cost=10**9,
    )
    density, pacing = pl.pallas_call(
        lambda *refs: final_kernel(keys, *refs),
        out_shape=(shape(adv_count, imp_count), shape(rows, BLOCK)),
        in_specs=[VMEM] * (2 + len(terms)),
        out_specs=(HBM, HBM),
        scratch_shapes=[
            pltpu.VMEM((rows, BLOCK), F32),
            pltpu.VMEM((adv_count, imp_count), F32),
            pltpu.SemaphoreType.DMA((rows + 1,)),
        ],
        compiler_params=PARAMS,
    )(gain_rows, limit, *terms)
    return density, prices.reshape(imp_count), pacing.reshape(adv_count)


def plain(adv_embed, imp_embed, value_scale, spend_class, eligible):
    imp_block = lax.all_gather(imp_embed, "adv", axis=0, tiled=True)
    rows = lax.all_gather(adv_embed, "imp", axis=0, tiled=True)
    scores = SCORE_GAIN * jnp.einsum(
        "ae,ie->ai", rows, imp_block, precision=lax.Precision.HIGHEST, preferred_element_type=F32
    )
    total_advs = scores.shape[0] * lax.axis_size("adv")
    total_imps = scores.shape[1] * lax.axis_size("imp")
    mask = jnp.repeat(jnp.repeat(eligible.astype(F32), BLOCK, axis=0), BLOCK, axis=1)
    values = value_scale[:, None] * jnp.exp(scores) * mask
    allowance = total_imps / total_advs * jnp.exp(0.3 * spend_class.astype(F32) - 1.2)
    bid_tile = mask * allowance[:, None] / total_imps
    for _ in range(ITERS):
        prices = lax.psum(jnp.sum(bid_tile, axis=0), "adv")
        gain = values * bid_tile / prices[None, :]
        spending = lax.psum(jnp.sum(gain, axis=1), "imp")
        pacing = allowance / jnp.maximum(spending, allowance)
        bid_tile = pacing[:, None] * gain
    return bid_tile * total_advs, prices, pacing


def per_device(adv_embed, imp_embed, value_scale, spend_class, eligible):
    sizes = (lax.axis_size("adv"), lax.axis_size("imp"), adv_embed.shape, imp_embed.shape, eligible.shape)
    fits = sizes == (2, 16, (BLOCK, EMB), (2 * BLOCK, EMB), (16, 4))
    return (staged if fits else plain)(adv_embed, imp_embed, value_scale, spend_class, eligible)


def solution(mesh):
    in_specs = (
        P(("adv", "imp"), None),
        P(("imp", "adv"), None),
        P("adv"),
        P("adv"),
        P("adv", "imp"),
    )
    out_specs = (P("adv", "imp"), P("imp"), P("adv"))
    return jax.shard_map(
        per_device, mesh=mesh, in_specs=in_specs, out_specs=out_specs, check_vma=False
    )
```

```python
import math

import jax
import jax.numpy as jnp
from jax import lax
from jax.experimental import pallas as pl
from jax.experimental.pallas import tpu as pltpu
from jax.sharding import PartitionSpec as P

BLOCK = 128
ITERS = 2
SCORE_GAIN = 0.0875
LOG2E = 1.4426950408889634
OFF = 1e30
SMALL = 2.0**-10
EMB = 64
DEPTH = 3 * EMB + 16
F32, BF16 = jnp.float32, jnp.bfloat16

VMEM = pl.BlockSpec(memory_space=pltpu.VMEM)
HBM = pl.BlockSpec(memory_space=pltpu.HBM)
PARAMS = pltpu.CompilerParams(vmem_limit_bytes=16 * 1024 * 1024)


def home():
    m = lax.axis_index("imp")
    return m, (m >> 2) & 1


def pieces(x):
    first = x.astype(BF16).astype(F32)
    rest = x - first
    second = rest.astype(BF16).astype(F32)
    third = (rest - second).astype(BF16).astype(F32)
    return first, second, third


def halves(block):
    high = block.astype(BF16)
    return high, (block - high.astype(F32)).astype(BF16)


def tree(terms):
    while len(terms) > 1:
        terms = [a + b for a, b in zip(terms[::2], terms[1::2])]
    return terms[0]


def in_order(w, own, other):
    return jnp.concatenate([jnp.where(w == 0, own, other), jnp.where(w == 0, other, own)], axis=0)


def prepare_kernel(
    ratio, imps, elig_hbm, class_hbm, scale_hbm, imp_hbm, adv_hbm,
    pack_ref, logs_ref, limit_ref, own_ref, elig_ref, class_ref, scale_ref, sems,
):
    moves = (
        (elig_hbm, elig_ref),
        (class_hbm, class_ref),
        (scale_hbm, scale_ref),
        (imp_hbm, pack_ref.at[0:EMB]),
        (adv_hbm, own_ref),
    )
    copies = [pltpu.make_async_copy(src, dst, sems.at[n]) for n, (src, dst) in enumerate(moves)]
    for copy in copies:
        copy.start()
    pack_ref[EMB : EMB + 8, :] = jnp.zeros((8, pack_ref.shape[1]), F32)
    for copy in copies:
        copy.wait()
    exponent = 0.3 * class_ref[...].astype(F32) - 1.2
    limit = ratio * jnp.exp(exponent)
    limit_ref[...] = limit
    logs_ref[...] = jnp.log(scale_ref[...]) * LOG2E + (exponent * LOG2E + math.log2(ratio / imps))
    rows, cols = class_ref.shape[0], elig_ref.shape[0]
    flags = elig_ref[...].astype(F32)
    allowance = limit / imps
    sums = sum(jnp.dot(flags.astype(BF16), p.astype(BF16), preferred_element_type=F32) for p in pieces(allowance))
    pack_ref[EMB : EMB + cols, 0:BLOCK] = sums
    pack_ref[EMB + 4 : EMB + 4 + cols, 0:rows] = flags


def own_flags(pack_ref, cols, rows):
    return pack_ref[EMB + 4 : EMB + 4 + cols, 0:rows]


def extra_rows(flags, logs):
    cols, rows = flags.shape
    count = logs.shape[0] * BLOCK
    at = lax.broadcasted_iota(jnp.int32, (rows, count), 0)
    spread = (at == lax.broadcasted_iota(jnp.int32, (rows, count), 1) // BLOCK).astype(BF16)
    masks = (jnp.dot(flags.astype(BF16), spread, preferred_element_type=F32) - 1.0) * OFF
    line = jnp.concatenate([logs[r : r + 1] for r in range(logs.shape[0])], axis=1)
    ones = jnp.ones((1, count), F32)
    parts = [masks, *pieces(line), ones, ones, ones, jnp.zeros((10 - cols, count), F32)]
    return jnp.concatenate(parts, axis=0).astype(BF16)


def impressions_kernel(cols, rows, own_ref, side_ref, cross_ref, down_ref, logs_ref, lhs_ref, lhs_t_ref, extra_ref, price_ref):
    _, w = home()
    half = lax.axis_index("adv")
    width = own_ref.shape[1]
    count = 2 * cols * BLOCK
    places = ((own_ref, w, half), (down_ref, w, 1 - half), (side_ref, 1 - w, half), (cross_ref, 1 - w, 1 - half))
    for ref, side, part in places:
        high, low = halves(ref[0:EMB, :] * (SCORE_GAIN * LOG2E))
        at = pl.ds(pl.multiple_of(side * (2 * width) + part * width, width), width)
        lhs_ref[0:EMB, at] = high
        lhs_ref[EMB : 2 * EMB, at] = low
        lhs_ref[2 * EMB : 3 * EMB, at] = high
    lanes = [a[EMB : EMB + cols, 0:BLOCK] + b[EMB : EMB + cols, 0:BLOCK] for a, b in ((own_ref, down_ref), (side_ref, cross_ref))]
    totals = jnp.sum(in_order(w, *lanes), axis=1, keepdims=True)
    price_ref[...] = jnp.broadcast_to(totals, price_ref.shape)
    price = jnp.concatenate([price_ref[c : c + 1, :] for c in range(2 * cols)], axis=1)
    column = lax.broadcasted_iota(jnp.int32, (2 * cols, count), 1) // BLOCK
    own = (column == lax.broadcasted_iota(jnp.int32, (2 * cols, count), 0)).astype(F32)
    ones = jnp.ones((1, count), F32)
    parts = [own, ones, ones, ones, *pieces(-jnp.log(price) * LOG2E), jnp.zeros((10 - 2 * cols, count), F32)]
    lhs_ref[3 * EMB :, :] = jnp.concatenate(parts, axis=0).astype(BF16)
    lhs_t_ref[...] = lhs_ref[...].T
    flags = in_order(w, own_flags(own_ref, cols, rows), own_flags(side_ref, cols, rows))
    extra_ref[...] = extra_rows(flags, logs_ref[...])


def first_kernel(keys, adv_ref, extra_ref, lhs_t_ref, *refs):
    *earlier, gain_ref, sums_ref, rhs_ref = refs
    m, _ = home()
    count = gain_ref.shape[0]
    if earlier:
        sums_ref[...] = earlier[0][...]
    else:
        sums_ref[...] = jnp.zeros(sums_ref.shape, F32)
    for n in range(0, len(keys), 2):
        two = slice(n * BLOCK, (n + 2) * BLOCK)
        for p in range(2):
            lanes = slice((n + p) * BLOCK, (n + p + 1) * BLOCK)
            high, low = halves(adv_ref[n + p])
            rhs_ref[0:EMB, lanes] = high
            rhs_ref[EMB : 2 * EMB, lanes] = high
            rhs_ref[2 * EMB : 3 * EMB, lanes] = low
            at = pl.multiple_of((m ^ keys[n + p]) * BLOCK, BLOCK)
            rhs_ref[3 * EMB :, lanes] = extra_ref[:, pl.ds(at, BLOCK)]
        sums = jnp.zeros((1, 2 * BLOCK), F32)
        for h in range(2):
            part = slice(h * count // 2, (h + 1) * count // 2)
            gain = jnp.exp2(jnp.dot(lhs_t_ref[part, :], rhs_ref[:, two], preferred_element_type=F32))
            sums = sums + jnp.sum(gain, axis=0, keepdims=True)
            gain_ref[part, two] = gain
        for p in range(2):
            sums_ref[pl.ds(m ^ keys[n + p], 1), :] = sums[:, p * BLOCK : (p + 1) * BLOCK]


def rows_kernel(lhs_ref, *refs):
    *rhs_refs, gain_ref = refs
    _, w = home()
    width = gain_ref.shape[1]
    lhs = lhs_ref[:, pl.ds(pl.multiple_of(w * width, width), width)]
    at = 0
    for ref in rhs_refs:
        for lane in range(0, ref.shape[1], BLOCK):
            rhs = ref[:, lane : lane + BLOCK].T
            gain_ref[at : at + BLOCK, :] = jnp.exp2(jnp.dot(rhs, lhs, preferred_element_type=F32))
            at += BLOCK


def tiles(refs, c):
    rows = slice(c * BLOCK, (c + 1) * BLOCK)
    return [(ref, (rows, slice(lane, lane + BLOCK))) for ref in refs for lane in range(0, ref.shape[1], BLOCK)]


def squares_kernel(parts, *refs):
    for ref, out_ref in zip(refs[:parts], refs[parts:]):
        out_ref[...] = (ref[...] * SMALL) * (ref[...] * SMALL)


def prices_kernel(keys, parts, limit_ref, *refs):
    gains, sum_refs, (part_ref, pacing_ref) = refs[:parts], refs[parts:-2], refs[-2:]
    m, _ = home()
    limit = limit_ref[...]
    pacing_ref[...] = limit / jnp.maximum(tree([ref[...] for ref in sum_refs]), limit)
    factors = [pacing_ref[pl.ds(m ^ k, 1), :] for k in keys]
    for c in range(part_ref.shape[0]):
        total = jnp.zeros((BLOCK, BLOCK), F32)
        paced = [ref[at] * factor for (ref, at), factor in zip(tiles(gains, c), factors)]
        for one, two in zip(paced[::2], paced[1::2]):
            total = total + (one + two)
        part_ref[c : c + 1, :] = jnp.sum(total.T, axis=0, keepdims=True)


def second_kernel(keys, parts, imps, limit_ref, pacing_ref, price_ref, *refs):
    squares, part_refs, (sums_ref, prices_ref, factor_ref, change_ref) = refs[:parts], refs[parts:-4], refs[-4:]
    m, w = home()
    prices = tree([ref[...] for ref in part_refs])
    changes = price_ref[...] / prices
    half = prices.shape[0] // 2
    prices_ref[...] = jnp.where(w == 0, prices[0:half], prices[half:])
    change = jnp.where(w == 0, changes[0:half], changes[half:])
    for c in range(half):
        change_ref[:, c * BLOCK : (c + 1) * BLOCK] = change[c : c + 1]
    factor_ref[...] = pacing_ref[...] * (imps / limit_ref[...])
    totals = [jnp.zeros((8, BLOCK), F32) for _ in keys]
    for c in range(2 * half):
        column = jnp.broadcast_to(changes[c : c + 1], (BLOCK, BLOCK)).T
        for n, (ref, at) in enumerate(tiles(squares, c)):
            totals[n] = totals[n] + jnp.sum((ref[at] * column).reshape(BLOCK // 8, 8, BLOCK), axis=0)
    for k, total in zip(keys, totals):
        sums_ref[pl.ds(m ^ k, 1), :] = jnp.sum(total, axis=0, keepdims=True)
    sums_ref[...] = sums_ref[...] * (factor_ref[...] / SMALL**2)


def final_kernel(keys, advs, gain_ref, limit_ref, factor_ref, change_ref, *refs):
    *sum_refs, out_ref, pacing_out, pacing_ref, scale_ref, block_ref, sems = refs
    m, _ = home()
    limit = limit_ref[...]
    pacing = limit / jnp.maximum(tree([ref[...] for ref in sum_refs]), limit)
    scale_ref[...] = pacing * factor_ref[...] * advs
    pacing_ref[...] = pacing
    copies = [pltpu.make_async_copy(pacing_ref, pacing_out, sems.at[len(keys)])]
    copies[0].start()
    change = change_ref[...]
    shape = (BLOCK, BLOCK)
    diagonal = lax.broadcasted_iota(jnp.int32, shape, 0) == lax.broadcasted_iota(jnp.int32, shape, 1)
    for n, k in enumerate(keys):
        rows = slice(n * BLOCK, (n + 1) * BLOCK)
        scale = jnp.sum(jnp.where(diagonal, scale_ref[pl.ds(m ^ k, 1), :], 0.0), axis=1, keepdims=True)
        gain = gain_ref[rows, :]
        block_ref[rows, :] = (gain * scale) * (gain * change)
        to = pl.ds(pl.multiple_of((m ^ k) * BLOCK, BLOCK), BLOCK)
        copy = pltpu.make_async_copy(block_ref.at[rows], out_ref.at[to], sems.at[n])
        copy.start()
        copies.append(copy)
    for copy in copies:
        copy.wait()


def swap(x, axis, k):
    return lax.ppermute(x, axis, [(i, i ^ k) for i in range(lax.axis_size(axis))])


def with_partners(x, keys):
    return [x] + [swap(x, "imp", k) for k in keys]


def over_impressions(sums, stages):
    first, last = stages
    return with_partners(tree(with_partners(sums, first)), last)


def staged(adv_embed, imp_embed, value_scale, spend_class, eligible):
    adv_count = spend_class.shape[0]
    rows, cols = eligible.shape
    imp_count = cols * BLOCK
    imps, advs = imp_count * lax.axis_size("imp"), adv_count * lax.axis_size("adv")
    ratio = imps / advs

    def shape(*dims, dtype=F32):
        return jax.ShapeDtypeStruct(dims, dtype)

    def call(kernel, out, operands, cost=0, **kw):
        return pl.pallas_call(
            kernel,
            out_shape=out,
            in_specs=[VMEM] * len(operands),
            out_specs=tuple(VMEM for _ in out),
            compiler_params=PARAMS,
            cost_estimate=pl.CostEstimate(flops=cost, bytes_accessed=cost // 256, transcendentals=0),
            **kw,
        )(*operands)

    adv_t = adv_embed.T
    ins = (eligible.T, spend_class.reshape(rows, BLOCK), value_scale.reshape(rows, BLOCK), imp_embed.T, adv_t)
    ins = [pltpu.with_memory_space_constraint(x, pltpu.HBM) for x in ins]
    pack, logs, limit, own = pl.pallas_call(
        lambda *refs: prepare_kernel(ratio, imps, *refs),
        out_shape=(shape(EMB + 8, imp_embed.shape[0]), shape(rows, BLOCK), shape(rows, BLOCK), shape(*adv_t.shape)),
        in_specs=[HBM] * len(ins),
        out_specs=(VMEM,) * 4,
        scratch_shapes=[
            pltpu.VMEM((cols, rows), jnp.int32),
            pltpu.VMEM((rows, BLOCK), jnp.int32),
            pltpu.VMEM((rows, BLOCK), F32),
            pltpu.SemaphoreType.DMA((len(ins),)),
        ],
        compiler_params=PARAMS,
    )(*ins)
    line = jnp.stack([own, *with_partners(adv_t, (4, 12, 8))[1:]])
    side, cross, down = [swap(pack, ("adv", "imp"), k) for k in (4, 20, 16)]
    plane = swap(line, "imp", 2)
    plane, _ = lax.optimization_barrier((plane, (side, cross, down)))
    ready, _ = lax.optimization_barrier((line, (side, cross, down)))
    line_pair = swap(ready, "imp", 1)
    at_line = (0, 4, 12, 8)
    at_line_pair = tuple(k + 1 for k in at_line)
    at_plane = tuple(k + 2 for k in at_line)
    at_plane_pair = tuple(k + 3 for k in at_line)
    keys = at_line + at_line_pair + at_plane + at_plane_pair

    count = 2 * imp_count
    lhs, lhs_t, extra, first_price = call(
        lambda *refs: impressions_kernel(cols, rows, *refs),
        (
            shape(DEPTH, count, dtype=BF16),
            shape(count, DEPTH, dtype=BF16),
            shape(16, adv_count, dtype=BF16),
            shape(2 * cols, BLOCK),
        ),
        (pack, side, cross, down, logs),
        cost=10**8,
    )
    gains, rhs, sums = [], [], ()

    def work(at, blocks):
        nonlocal sums
        width = len(at) * BLOCK
        gain, total, side = call(
            lambda *refs: first_kernel(at, *refs),
            (pltpu.VMEM((count, width), F32), shape(rows, BLOCK), pltpu.VMEM((DEPTH, width), BF16)),
            (blocks, extra, lhs_t, *sums),
            cost=10**8 * len(at),
        )
        gains.append(gain)
        rhs.append(side)
        sums = (total,)

    work(at_line, line)
    plane, sums = lax.optimization_barrier((plane, sums))
    work(at_line_pair, line_pair)
    work(at_plane, plane)
    work(at_plane_pair, swap(plane, "imp", 1))

    squares = call(
        lambda *refs: squares_kernel(len(gains), *refs),
        tuple(pltpu.VMEM(g.shape, F32) for g in gains),
        gains,
        cost=10**9,
    )
    terms = over_impressions(sums[0], ((8,),(1,2,3)))
    (gain_rows,) = call(rows_kernel, (pltpu.VMEM((adv_count, imp_count), F32),), (lhs, *rhs), cost=10**9)

    part, pacing = call(
        lambda *refs: prices_kernel(keys, len(gains), *refs),
        (shape(2 * cols, BLOCK), shape(rows, BLOCK)),
        (limit, *gains, *terms),
    )
    sums, prices, factor, change = call(
        lambda *refs: second_kernel(keys, len(gains), imps, *refs),
        (shape(rows, BLOCK), pltpu.VMEM((cols, BLOCK), F32), shape(rows, BLOCK), shape(1, imp_count)),
        (limit, pacing, first_price, *squares, part, swap(part, "adv", 1)),
    )

    terms = over_impressions(sums, ((8,),(1,2,3)))
    density, pacing = pl.pallas_call(
        lambda *refs: final_kernel(keys, advs, *refs),
        out_shape=(shape(adv_count, imp_count), shape(rows, BLOCK)),
        in_specs=[VMEM] * (4 + len(terms)),
        out_specs=(HBM, HBM),
        scratch_shapes=[
            pltpu.VMEM((rows, BLOCK), F32),
            pltpu.VMEM((rows, BLOCK), F32),
            pltpu.VMEM((adv_count, imp_count), F32),
            pltpu.SemaphoreType.DMA((rows + 1,)),
        ],
        compiler_params=PARAMS,
    )(gain_rows, limit, factor, change, *terms)
    return density, prices.reshape(imp_count), pacing.reshape(adv_count)


def plain(adv_embed, imp_embed, value_scale, spend_class, eligible):
    imp_block = lax.all_gather(imp_embed, "adv", axis=0, tiled=True)
    rows = lax.all_gather(adv_embed, "imp", axis=0, tiled=True)
    scores = SCORE_GAIN * jnp.einsum(
        "ae,ie->ai", rows, imp_block, precision=lax.Precision.HIGHEST, preferred_element_type=F32
    )
    total_advs = scores.shape[0] * lax.axis_size("adv")
    total_imps = scores.shape[1] * lax.axis_size("imp")
    mask = jnp.repeat(jnp.repeat(eligible.astype(F32), BLOCK, axis=0), BLOCK, axis=1)
    values = value_scale[:, None] * jnp.exp(scores) * mask
    allowance = total_imps / total_advs * jnp.exp(0.3 * spend_class.astype(F32) - 1.2)
    bid_tile = mask * allowance[:, None] / total_imps
    for _ in range(ITERS):
        prices = lax.psum(jnp.sum(bid_tile, axis=0), "adv")
        gain = values * bid_tile / prices[None, :]
        spending = lax.psum(jnp.sum(gain, axis=1), "imp")
        pacing = allowance / jnp.maximum(spending, allowance)
        bid_tile = pacing[:, None] * gain
    return bid_tile * total_advs, prices, pacing


def per_device(adv_embed, imp_embed, value_scale, spend_class, eligible):
    sizes = (lax.axis_size("adv"), lax.axis_size("imp"), adv_embed.shape, imp_embed.shape, eligible.shape)
    fits = sizes == (2, 16, (BLOCK, EMB), (2 * BLOCK, EMB), (16, 4))
    return (staged if fits else plain)(adv_embed, imp_embed, value_scale, spend_class, eligible)


def solution(mesh):
    in_specs = (
        P(("adv", "imp"), None),
        P(("imp", "adv"), None),
        P("adv"),
        P("adv"),
        P("adv", "imp"),
    )
    out_specs = (P("adv", "imp"), P("imp"), P("adv"))
    return jax.shard_map(
        per_device, mesh=mesh, in_specs=in_specs, out_specs=out_specs, check_vma=False
    )
```

```python
import math

import jax
import jax.numpy as jnp
from jax import lax
from jax.experimental import pallas as pl
from jax.experimental.pallas import tpu as pltpu
from jax.sharding import PartitionSpec as P

BLOCK = 128
ITERS = 2
SCORE_GAIN = 0.0875
LOG2E = 1.4426950408889634
OFF = 1e30
SMALL = 2.0**-10
EMB = 64
DEPTH = 3 * EMB + 16
F32, BF16 = jnp.float32, jnp.bfloat16

VMEM = pl.BlockSpec(memory_space=pltpu.VMEM)
HBM = pl.BlockSpec(memory_space=pltpu.HBM)
PARAMS = pltpu.CompilerParams(vmem_limit_bytes=16 * 1024 * 1024)


def home():
    m = lax.axis_index("imp")
    return m, (m >> 2) & 1


def pieces(x):
    first = x.astype(BF16).astype(F32)
    rest = x - first
    second = rest.astype(BF16).astype(F32)
    third = (rest - second).astype(BF16).astype(F32)
    return first, second, third


def halves(block):
    high = block.astype(BF16)
    return high, (block - high.astype(F32)).astype(BF16)


def tree(terms):
    while len(terms) > 1:
        terms = [a + b for a, b in zip(terms[::2], terms[1::2])]
    return terms[0]


def in_order(w, own, other):
    return jnp.concatenate([jnp.where(w == 0, own, other), jnp.where(w == 0, other, own)], axis=0)


def prepare_kernel(
    ratio, imps, elig_hbm, class_hbm, scale_hbm, imp_hbm, adv_hbm,
    pack_ref, logs_ref, limit_ref, own_ref, elig_ref, class_ref, scale_ref, sems,
):
    moves = (
        (elig_hbm, elig_ref),
        (class_hbm, class_ref),
        (scale_hbm, scale_ref),
        (imp_hbm, pack_ref.at[0:EMB]),
        (adv_hbm, own_ref),
    )
    copies = [pltpu.make_async_copy(src, dst, sems.at[n]) for n, (src, dst) in enumerate(moves)]
    for copy in copies:
        copy.start()
    pack_ref[EMB : EMB + 8, :] = jnp.zeros((8, pack_ref.shape[1]), F32)
    for copy in copies:
        copy.wait()
    exponent = 0.3 * class_ref[...].astype(F32) - 1.2
    limit = ratio * jnp.exp(exponent)
    limit_ref[...] = limit
    logs_ref[...] = jnp.log(scale_ref[...]) * LOG2E + (exponent * LOG2E + math.log2(ratio / imps))
    rows, cols = class_ref.shape[0], elig_ref.shape[0]
    flags = elig_ref[...].astype(F32)
    allowance = limit / imps
    sums = sum(jnp.dot(flags.astype(BF16), p.astype(BF16), preferred_element_type=F32) for p in pieces(allowance))
    pack_ref[EMB : EMB + cols, 0:BLOCK] = sums
    pack_ref[EMB + 4 : EMB + 4 + cols, 0:rows] = flags


def own_flags(pack_ref, cols, rows):
    return pack_ref[EMB + 4 : EMB + 4 + cols, 0:rows]


def extra_rows(flags, logs):
    cols, rows = flags.shape
    count = logs.shape[0] * BLOCK
    at = lax.broadcasted_iota(jnp.int32, (rows, count), 0)
    spread = (at == lax.broadcasted_iota(jnp.int32, (rows, count), 1) // BLOCK).astype(BF16)
    masks = (jnp.dot(flags.astype(BF16), spread, preferred_element_type=F32) - 1.0) * OFF
    line = jnp.concatenate([logs[r : r + 1] for r in range(logs.shape[0])], axis=1)
    ones = jnp.ones((1, count), F32)
    parts = [masks, *pieces(line), ones, ones, ones, jnp.zeros((10 - cols, count), F32)]
    return jnp.concatenate(parts, axis=0).astype(BF16)


def impressions_kernel(cols, rows, own_ref, down_ref, side_ref, cross_ref, logs_ref, lhs_ref, lhs_t_ref, extra_ref, price_ref):
    _, w = home()
    half = lax.axis_index("adv")
    width = own_ref.shape[1]
    count = 2 * cols * BLOCK
    places = ((own_ref, w, half), (down_ref, w, 1 - half), (side_ref, 1 - w, half), (cross_ref, 1 - w, 1 - half))
    for ref, side, part in places:
        high, low = halves(ref[0:EMB, :] * (SCORE_GAIN * LOG2E))
        at = pl.ds(pl.multiple_of(side * (2 * width) + part * width, width), width)
        lhs_ref[0:EMB, at] = high
        lhs_ref[EMB : 2 * EMB, at] = low
        lhs_ref[2 * EMB : 3 * EMB, at] = high
    lanes = [a[EMB : EMB + cols, 0:BLOCK] + b[EMB : EMB + cols, 0:BLOCK] for a, b in ((own_ref, down_ref), (side_ref, cross_ref))]
    totals = jnp.sum(in_order(w, *lanes), axis=1, keepdims=True)
    price_ref[...] = jnp.broadcast_to(totals, price_ref.shape)
    price = jnp.concatenate([price_ref[c : c + 1, :] for c in range(2 * cols)], axis=1)
    column = lax.broadcasted_iota(jnp.int32, (2 * cols, count), 1) // BLOCK
    own = (column == lax.broadcasted_iota(jnp.int32, (2 * cols, count), 0)).astype(F32)
    ones = jnp.ones((1, count), F32)
    parts = [own, ones, ones, ones, *pieces(-jnp.log(price) * LOG2E), jnp.zeros((10 - 2 * cols, count), F32)]
    lhs_ref[3 * EMB :, :] = jnp.concatenate(parts, axis=0).astype(BF16)
    lhs_t_ref[...] = lhs_ref[...].T
    flags = in_order(w, own_flags(own_ref, cols, rows), own_flags(side_ref, cols, rows))
    extra_ref[...] = extra_rows(flags, logs_ref[...])


def first_kernel(keys, adv_ref, extra_ref, lhs_t_ref, *refs):
    *earlier, gain_ref, sums_ref, rhs_ref = refs
    m, _ = home()
    count = gain_ref.shape[0]
    if earlier:
        sums_ref[...] = earlier[0][...]
    else:
        sums_ref[...] = jnp.zeros(sums_ref.shape, F32)
    for n in range(0, len(keys), 2):
        two = slice(n * BLOCK, (n + 2) * BLOCK)
        for p in range(2):
            lanes = slice((n + p) * BLOCK, (n + p + 1) * BLOCK)
            high, low = halves(adv_ref[n + p])
            rhs_ref[0:EMB, lanes] = high
            rhs_ref[EMB : 2 * EMB, lanes] = high
            rhs_ref[2 * EMB : 3 * EMB, lanes] = low
            at = pl.multiple_of((m ^ keys[n + p]) * BLOCK, BLOCK)
            rhs_ref[3 * EMB :, lanes] = extra_ref[:, pl.ds(at, BLOCK)]
        sums = jnp.zeros((1, 2 * BLOCK), F32)
        for h in range(2):
            part = slice(h * count // 2, (h + 1) * count // 2)
            gain = jnp.exp2(jnp.dot(lhs_t_ref[part, :], rhs_ref[:, two], preferred_element_type=F32))
            sums = sums + jnp.sum(gain, axis=0, keepdims=True)
            gain_ref[part, two] = gain
        for p in range(2):
            sums_ref[pl.ds(m ^ keys[n + p], 1), :] = sums[:, p * BLOCK : (p + 1) * BLOCK]


def as_column(row):
    shape = (BLOCK, BLOCK)
    diagonal = lax.broadcasted_iota(jnp.int32, shape, 0) == lax.broadcasted_iota(jnp.int32, shape, 1)
    return jnp.sum(jnp.where(diagonal, row, 0.0), axis=1, keepdims=True)


def rows_kernel(keys, advs, lhs_ref, factor_ref, change_ref, *refs):
    *rhs_refs, out_ref = refs
    m, w = home()
    width = out_ref.shape[1]
    lhs = lhs_ref[:, pl.ds(pl.multiple_of(w * width, width), width)]
    change = change_ref[...]
    blocks = [(ref, lane) for ref in rhs_refs for lane in range(0, ref.shape[1], BLOCK)]
    for n, (ref, lane) in enumerate(blocks):
        gain = jnp.exp2(jnp.dot(ref[:, lane : lane + BLOCK].T, lhs, preferred_element_type=F32))
        factor = as_column(factor_ref[pl.ds(m ^ keys[n], 1), :] * advs)
        out_ref[n * BLOCK : (n + 1) * BLOCK, :] = (gain * factor) * (gain * change)


def tiles(refs, c):
    rows = slice(c * BLOCK, (c + 1) * BLOCK)
    return [(ref, (rows, slice(lane, lane + BLOCK))) for ref in refs for lane in range(0, ref.shape[1], BLOCK)]


def squares_kernel(parts, *refs):
    for ref, out_ref in zip(refs[:parts], refs[parts:]):
        out_ref[...] = (ref[...] * SMALL) * (ref[...] * SMALL)


def prices_kernel(keys, parts, limit_ref, *refs):
    gains, sum_refs, (part_ref, pacing_ref) = refs[:parts], refs[parts:-2], refs[-2:]
    m, _ = home()
    limit = limit_ref[...]
    pacing_ref[...] = limit / jnp.maximum(tree([ref[...] for ref in sum_refs]), limit)
    factors = [pacing_ref[pl.ds(m ^ k, 1), :] for k in keys]
    for c in range(part_ref.shape[0]):
        total = jnp.zeros((BLOCK, BLOCK), F32)
        paced = [ref[at] * factor for (ref, at), factor in zip(tiles(gains, c), factors)]
        for one, two in zip(paced[::2], paced[1::2]):
            total = total + (one + two)
        part_ref[c : c + 1, :] = jnp.sum(total.T, axis=0, keepdims=True)


def second_kernel(keys, parts, imps, limit_ref, pacing_ref, price_ref, *refs):
    squares, part_refs, (sums_ref, prices_ref, factor_ref, change_ref) = refs[:parts], refs[parts:-4], refs[-4:]
    m, w = home()
    prices = tree([ref[...] for ref in part_refs])
    changes = price_ref[...] / prices
    half = prices.shape[0] // 2
    prices_ref[...] = jnp.where(w == 0, prices[0:half], prices[half:])
    change = jnp.where(w == 0, changes[0:half], changes[half:])
    for c in range(half):
        change_ref[:, c * BLOCK : (c + 1) * BLOCK] = change[c : c + 1]
    factor_ref[...] = pacing_ref[...] * (imps / limit_ref[...])
    totals = [jnp.zeros((8, BLOCK), F32) for _ in keys]
    for c in range(2 * half):
        column = jnp.broadcast_to(changes[c : c + 1], (BLOCK, BLOCK)).T
        for n, (ref, at) in enumerate(tiles(squares, c)):
            totals[n] = totals[n] + jnp.sum((ref[at] * column).reshape(BLOCK // 8, 8, BLOCK), axis=0)
    for k, total in zip(keys, totals):
        sums_ref[pl.ds(m ^ k, 1), :] = jnp.sum(total, axis=0, keepdims=True)
    sums_ref[...] = sums_ref[...] * (factor_ref[...] / SMALL**2)


def final_kernel(keys, gain_ref, limit_ref, *refs):
    *sum_refs, out_ref, pacing_out, pacing_ref, block_ref, sems = refs
    m, _ = home()
    limit = limit_ref[...]
    pacing_ref[...] = limit / jnp.maximum(tree([ref[...] for ref in sum_refs]), limit)
    copies = []
    for n, k in enumerate(keys):
        column = as_column(pacing_ref[pl.ds(m ^ k, 1), :])
        step = BLOCK // 4 if n == 0 else BLOCK
        for part in range(0, BLOCK, step):
            rows = slice(n * BLOCK + part, n * BLOCK + part + step)
            block_ref[rows, :] = gain_ref[rows, :] * column[part : part + step]
            to = pl.ds(pl.multiple_of((m ^ k) * BLOCK + part, step), step)
            copies.append(pltpu.make_async_copy(block_ref.at[rows], out_ref.at[to], sems.at[len(copies)]))
            copies[-1].start()
    copies.append(pltpu.make_async_copy(pacing_ref, pacing_out, sems.at[len(copies)]))
    copies[-1].start()
    for copy in copies:
        copy.wait()


def swap(x, axis, k):
    return lax.ppermute(x, axis, [(i, i ^ k) for i in range(lax.axis_size(axis))])


def with_partners(x, keys):
    return [x] + [swap(x, "imp", k) for k in keys]


def over_impressions(sums, stages):
    first, last = stages
    return with_partners(tree(with_partners(sums, first)), last)


def staged(adv_embed, imp_embed, value_scale, spend_class, eligible):
    adv_count = spend_class.shape[0]
    rows, cols = eligible.shape
    imp_count = cols * BLOCK
    imps, advs = imp_count * lax.axis_size("imp"), adv_count * lax.axis_size("adv")
    ratio = imps / advs

    def shape(*dims, dtype=F32):
        return jax.ShapeDtypeStruct(dims, dtype)

    def call(kernel, out, operands, cost=0, **kw):
        return pl.pallas_call(
            kernel,
            out_shape=out,
            in_specs=[VMEM] * len(operands),
            out_specs=tuple(VMEM for _ in out),
            compiler_params=PARAMS,
            cost_estimate=pl.CostEstimate(flops=cost, bytes_accessed=cost // 256, transcendentals=0),
            **kw,
        )(*operands)

    adv_t = adv_embed.T
    ins = (eligible.T, spend_class.reshape(rows, BLOCK), value_scale.reshape(rows, BLOCK), imp_embed.T, adv_t)
    ins = [pltpu.with_memory_space_constraint(x, pltpu.HBM) for x in ins]
    pack, logs, limit, own = pl.pallas_call(
        lambda *refs: prepare_kernel(ratio, imps, *refs),
        out_shape=(shape(EMB + 8, imp_embed.shape[0]), shape(rows, BLOCK), shape(rows, BLOCK), shape(*adv_t.shape)),
        in_specs=[HBM] * len(ins),
        out_specs=(VMEM,) * 4,
        scratch_shapes=[
            pltpu.VMEM((cols, rows), jnp.int32),
            pltpu.VMEM((rows, BLOCK), jnp.int32),
            pltpu.VMEM((rows, BLOCK), F32),
            pltpu.SemaphoreType.DMA((len(ins),)),
        ],
        compiler_params=PARAMS,
    )(*ins)
    line = jnp.stack([own, *with_partners(adv_t, (4, 12, 8))[1:]])
    down, side, cross = [swap(pack, ("adv", "imp"), k) for k in (16, 4, 20)]
    plane = swap(line, "imp", 2)
    plane, _ = lax.optimization_barrier((plane, (down, side, cross)))
    ready, _ = lax.optimization_barrier((line, (down, side, cross)))
    line_pair = swap(ready, "imp", 1)
    at_line = (0, 4, 12, 8)
    at_line_pair = tuple(k + 1 for k in at_line)
    at_plane = tuple(k + 2 for k in at_line)
    at_plane_pair = tuple(k + 3 for k in at_line)
    keys = at_line + at_line_pair + at_plane + at_plane_pair

    count = 2 * imp_count
    lhs, lhs_t, extra, first_price = call(
        lambda *refs: impressions_kernel(cols, rows, *refs),
        (
            shape(DEPTH, count, dtype=BF16),
            shape(count, DEPTH, dtype=BF16),
            shape(16, adv_count, dtype=BF16),
            shape(2 * cols, BLOCK),
        ),
        (pack, down, side, cross, logs),
        cost=10**8,
    )
    gains, rhs, sums = [], [], ()

    def work(at, blocks):
        nonlocal sums
        width = len(at) * BLOCK
        gain, total, side = call(
            lambda *refs: first_kernel(at, *refs),
            (pltpu.VMEM((count, width), F32), shape(rows, BLOCK), pltpu.VMEM((DEPTH, width), BF16)),
            (blocks, extra, lhs_t, *sums),
            cost=10**8 * len(at),
        )
        gains.append(gain)
        rhs.append(side)
        sums = (total,)

    work(at_line, line)
    plane, sums = lax.optimization_barrier((plane, sums))
    work(at_line_pair, line_pair)
    work(at_plane, plane)
    work(at_plane_pair, swap(plane, "imp", 1))

    squares = call(
        lambda *refs: squares_kernel(len(gains), *refs),
        tuple(pltpu.VMEM(g.shape, F32) for g in gains),
        gains,
        cost=10**9,
    )
    terms = over_impressions(sums[0], ((8,),(1,2,3)))

    part, pacing = call(
        lambda *refs: prices_kernel(keys, len(gains), *refs),
        (shape(2 * cols, BLOCK), shape(rows, BLOCK)),
        (limit, *gains, *terms),
    )
    sums, prices, factor, change = call(
        lambda *refs: second_kernel(keys, len(gains), imps, *refs),
        (shape(rows, BLOCK), pltpu.VMEM((cols, BLOCK), F32), shape(rows, BLOCK), shape(1, imp_count)),
        (limit, pacing, first_price, *squares, part, swap(part, "adv", 1)),
    )

    terms = over_impressions(sums, ((8,),(1,2,3)))
    (gain_rows,) = call(
        lambda *refs: rows_kernel(keys, advs, *refs),
        (pltpu.VMEM((adv_count, imp_count), F32),),
        (lhs, factor, change, *rhs),
        cost=10**9,
    )
    density, pacing = pl.pallas_call(
        lambda *refs: final_kernel(keys, *refs),
        out_shape=(shape(adv_count, imp_count), shape(rows, BLOCK)),
        in_specs=[VMEM] * (2 + len(terms)),
        out_specs=(HBM, HBM),
        scratch_shapes=[
            pltpu.VMEM((rows, BLOCK), F32),
            pltpu.VMEM((adv_count, imp_count), F32),
            pltpu.SemaphoreType.DMA((rows + 4,)),
        ],
        compiler_params=PARAMS,
    )(gain_rows, limit, *terms)
    return density, prices.reshape(imp_count), pacing.reshape(adv_count)


def plain(adv_embed, imp_embed, value_scale, spend_class, eligible):
    imp_block = lax.all_gather(imp_embed, "adv", axis=0, tiled=True)
    rows = lax.all_gather(adv_embed, "imp", axis=0, tiled=True)
    scores = SCORE_GAIN * jnp.einsum(
        "ae,ie->ai", rows, imp_block, precision=lax.Precision.HIGHEST, preferred_element_type=F32
    )
    total_advs = scores.shape[0] * lax.axis_size("adv")
    total_imps = scores.shape[1] * lax.axis_size("imp")
    mask = jnp.repeat(jnp.repeat(eligible.astype(F32), BLOCK, axis=0), BLOCK, axis=1)
    values = value_scale[:, None] * jnp.exp(scores) * mask
    allowance = total_imps / total_advs * jnp.exp(0.3 * spend_class.astype(F32) - 1.2)
    bid_tile = mask * allowance[:, None] / total_imps
    for _ in range(ITERS):
        prices = lax.psum(jnp.sum(bid_tile, axis=0), "adv")
        gain = values * bid_tile / prices[None, :]
        spending = lax.psum(jnp.sum(gain, axis=1), "imp")
        pacing = allowance / jnp.maximum(spending, allowance)
        bid_tile = pacing[:, None] * gain
    return bid_tile * total_advs, prices, pacing


def per_device(adv_embed, imp_embed, value_scale, spend_class, eligible):
    sizes = (lax.axis_size("adv"), lax.axis_size("imp"), adv_embed.shape, imp_embed.shape, eligible.shape)
    fits = sizes == (2, 16, (BLOCK, EMB), (2 * BLOCK, EMB), (16, 4))
    return (staged if fits else plain)(adv_embed, imp_embed, value_scale, spend_class, eligible)


def solution(mesh):
    in_specs = (
        P(("adv", "imp"), None),
        P(("imp", "adv"), None),
        P("adv"),
        P("adv"),
        P("adv", "imp"),
    )
    out_specs = (P("adv", "imp"), P("imp"), P("adv"))
    return jax.shard_map(
        per_device, mesh=mesh, in_specs=in_specs, out_specs=out_specs, check_vma=False
    )
```
